256 devices in a mesh: ctx: 32 (over z, y_hi, core), tp: 8 (over x, y_lo).
Axes of the slice: x: 4, y: 4 (y_hi: 2, y_lo: 2; y = y_hi * 2 + y_lo), z: 8, core: 2. Of those that a mesh axis runs over, the one named last changes fastest.
Arguments:
- qkv: bfloat16 [4096, 32, 3, 128], P('ctx', 'tp'), may hold values from -5 to 5
- grad_out: bfloat16 [4096, 8192], P(('ctx', 'tp')), may hold values from -6 to 6
- attn_out: bfloat16 [4096, 8192], P('tp'), may hold values from -0.09375 to 0.09375
Outputs:
- mixed_out: float32 [4096, 8192], P(('ctx', 'tp'))
- grad_qkv: float32 [4096, 32, 3, 128], P('ctx', 'tp')
The draws below stay inside these ranges and needn't reach their ends.
All inputs are finite; a program needn't handle non-finite values.
Results may differ from the reference program's by a relative error of at most 0.0063.
Values may be sent and summed in bfloat16 or wider, within the bound.
A program may use at most 128 MiB of HBM per device.

```python
import math
import jax
import jax.numpy as jnp
from jax import lax

D = 8192
HD = 128
HEADS = 32
SEQ = 4096


def draw_qkv(key, part):
    keys_all = jax.random.split(key, 1)
    full_shape = (SEQ, HEADS, 3, HD)
    return jnp.clip(jax.random.normal(keys_all[0], full_shape, jnp.float32), -5.0, 5.0).astype(jnp.bfloat16)


def block_levels(stream_key, extent, shards, low, high):
    def one(axis_at, shards_of):
        steps = jax.random.uniform(jax.random.fold_in(jax.random.fold_in(stream_key, 6), axis_at), (shards_of,), jnp.float32, low / len(shards), high / len(shards))
        return jnp.repeat(jnp.exp(steps), extent[axis_at] // shards_of).reshape((-1,) + (1,) * (len(extent) - axis_at - 1))

    level = one(*shards[0])
    for cut in shards[1:]:
        level = level * one(*cut)
    return level


def normal_values(own_key, shape, width, limit, cuts=(), kind=jnp.bfloat16):
    result = width * jax.random.normal(own_key, shape, jnp.float32)
    if cuts:
        result = result * block_levels(own_key, shape, cuts, -0.22, 0.18)
    return jnp.clip(result, -limit, limit).astype(kind)


def setup_inputs(seed: int = 0) -> dict:
    arg_keys = jax.random.split(jax.random.key(seed), 4)
    return {
        "qkv": draw_qkv(jax.random.fold_in(arg_keys[3], 71), 0),
        "grad_out": normal_values(arg_keys[1], (SEQ, D), 1.0, 6.0, ((0, 256),)),
        "attn_out": normal_values(arg_keys[2], (HEADS * HD, D), (HEADS * HD) ** -0.5, 0.09375, ((0, 8),)),
    }


def head_pass(operands):
    queries, keys_in, values_in, grad_att = operands
    factor = 1.0 / math.sqrt(HD)
    positions = jnp.arange(queries.shape[0], dtype=jnp.int32)
    visible = positions[None, :] <= positions[:, None]
    scores = jnp.dot(queries, keys_in.T, preferred_element_type=jnp.float32) * factor
    scores = jnp.where(visible, scores, -jnp.inf)
    row_max = lax.optimization_barrier(jnp.max(scores, axis=1, keepdims=True))
    log_total = row_max + jnp.log(lax.optimization_barrier(jnp.sum(jnp.exp(scores - row_max), axis=1, keepdims=True)))
    weights = jnp.exp(scores - log_total)
    weights_low = weights.astype(jnp.bfloat16)
    attended = jnp.dot(weights_low, values_in, preferred_element_type=jnp.float32).astype(jnp.bfloat16)
    row_delta = lax.optimization_barrier(jnp.sum(grad_att.astype(jnp.float32) * attended.astype(jnp.float32), axis=1, keepdims=True))
    grad_weights = jnp.dot(grad_att, values_in.T, preferred_element_type=jnp.float32)
    grad_scores = (weights * (grad_weights - row_delta) * factor).astype(jnp.bfloat16)
    grad_queries = jnp.dot(grad_scores, keys_in, preferred_element_type=jnp.float32)
    grad_keys = jnp.dot(grad_scores.T, queries, preferred_element_type=jnp.float32)
    grad_values = jnp.dot(weights_low.T, grad_att, preferred_element_type=jnp.float32)
    return (attended, grad_queries, grad_keys, grad_values)

def reference(qkv, grad_out, attn_out):
    seq_total = qkv.shape[0]
    queries = qkv[:, :, 0].transpose(1, 0, 2)
    keys_in = qkv[:, :, 1].transpose(1, 0, 2)
    values_in = qkv[:, :, 2].transpose(1, 0, 2)
    grad_full = jnp.dot(grad_out, attn_out.T, preferred_element_type=jnp.float32).astype(jnp.bfloat16)
    grad_att = grad_full.reshape(seq_total, HEADS, HD).transpose(1, 0, 2)
    attended, grad_queries, grad_keys, grad_values = lax.map(head_pass, (queries, keys_in, values_in, grad_att))
    attended_flat = attended.transpose(1, 0, 2).reshape(seq_total, HEADS * HD)
    mixed_out = jnp.dot(attended_flat, attn_out, preferred_element_type=jnp.float32)
    grad_qkv = jnp.stack([grad_queries, grad_keys, grad_values], axis=2).transpose(1, 0, 2, 3)
    return (mixed_out, grad_qkv)
```

```python
import functools
import math

import jax
import jax.numpy as jnp
from jax import lax
from jax.experimental import pallas as pl
from jax.experimental.pallas import tpu as pltpu
from jax.sharding import PartitionSpec as P

HD = 128
MESH = pl.DeviceIdType.MESH
F32 = jnp.float32
BF16 = jnp.bfloat16
D = 8192
CA = 2048
HALF = D // 2
NT = (((1,), (1,)), ((), ()))
TN = (((0,), (0,)), ((), ()))
NN = (((1,), (0,)), ((), ()))


def dot(a, b, dims):
    return lax.dot_general(a, b, dims, preferred_element_type=F32)


def kernel(
    qkv, go, wo,
    mixed, gqkv,
    w, g, kvb, qb, st, wl, dsb, ot, dqt, gs, gb, asend, ah,
    dkv, sb1, rb1, sb2, rb2, sb3, hb, sbq, hq,
    mf, mb, ra, sa, ra2, rb, sb, rbb,
    lsem, p1s, p1r, p2s, p2r, a1s, a1r, gts, gtr, ats, atr, c1s, c1r, c2s, c2r, c3s, c3r, dqs, dqr,
    mas, mar, ma2s, ma2r, mbs, mbr, mb2s, mb2r,
):
    ctx = lax.axis_index("ctx")
    tp = lax.axis_index("tp")
    h = ctx // 8
    k = ctx % 8
    zb = k // 4
    yh = (k // 2) % 2
    c = k % 2
    x = tp // 2
    yl = tp % 2
    chip = k // 2
    factor = 1.0 / math.sqrt(HD)

    heads_dev = {o: (((h + o) % 4) * 8 + k, tp) for o in (1, 2, 3)}
    core_dev = (ctx + 1 - 2 * c, tp)
    group = [
        (ctx + 4 - 8 * zb, tp),
        (ctx + 2 - 4 * yh, tp),
        (ctx + 6 - 8 * zb - 4 * yh, tp),
    ]
    group_chip = [chip + 2 - 4 * zb, chip + 1 - 2 * yh, 3 - chip]
    x_dev = {d: (ctx, ((x + d) % 4) * 2 + yl) for d in (1, 2, 3)}
    y_dev = (ctx, x * 2 + 1 - yl)

    w_cp = pltpu.make_async_copy(wo, w, lsem.at[0])
    w_cp.start()
    kv_cp = pltpu.make_async_copy(qkv.at[pl.ds(1, 2), h], kvb.at[:, h, k], lsem.at[1])
    kv_cp.start()
    q_cp = pltpu.make_async_copy(qkv.at[0, h], qb.at[h], lsem.at[2])
    q_cp.start()
    g_cp = pltpu.make_async_copy(go, g.at[tp], lsem.at[3])
    g_cp.start()

    barrier = pltpu.get_barrier_semaphore()
    everyone = list(heads_dev.values()) + [core_dev] + group + list(x_dev.values()) + [y_dev]
    for dev in everyone:
        pl.semaphore_signal(barrier, inc=1, device_id=dev, device_id_type=MESH)
    pl.semaphore_wait(barrier, len(everyone))

    sends = []

    def send(src, dst, ssem, rsem, dev):
        cp = pltpu.make_async_remote_copy(
            src_ref=src, dst_ref=dst, send_sem=ssem, recv_sem=rsem, device_id=dev, device_id_type=MESH
        )
        cp.start()
        sends.append(cp)
        return cp

    p1 = {}
    for o in (1, 3, 2):
        hh = (h + o) % 4
        p1[o] = send(
            qkv.at[pl.ds(1, 2), hh], kvb.at[:, h, k], p1s.at[0, o - 1], p1r.at[0, o - 1], heads_dev[o]
        )
    a1 = {}

    def a1_send(i, src, dst, dev):
        a1[i] = send(src, dst, a1s.at[i], a1r.at[i], dev)

    a1_send(0, go, g.at[tp], y_dev)
    a1_send(1, go, g.at[tp], x_dev[1])
    a1_send(2, go, g.at[tp], x_dev[3])
    p1q = {}
    for o in (1, 3, 2):
        hh = (h + o) % 4
        p1q[o] = send(qkv.at[0, hh], qb.at[h], p1s.at[1, o - 1], p1r.at[1, o - 1], heads_dev[o])

    p2 = {}

    def p2_block(o):
        s = (h + 4 - o) % 4
        part = kvb.at[:, s, k]
        for p in range(3):
            p2[p, o] = send(part, part, p2s.at[p, o], p2r.at[p, o], group[p])
        p2[3, o] = send(part, part, p2s.at[3, o], p2r.at[3, o], core_dev)

    def p2_forward(p, o):
        s = (h + 4 - o) % 4
        p2[p, o].wait_recv()
        part = kvb.at[:, s, group_chip[p] * 2 + c]
        p2[4 + p, o] = send(part, part, p2s.at[4 + p, o], p2r.at[4 + p, o], core_dev)

    kv_cp.wait()
    p2_block(0)
    p1[1].wait_recv()
    p2_block(1)
    p1[3].wait_recv()
    p2_block(3)
    a1[0].wait_recv()
    ty = x * 2 + 1 - yl
    a1_send(3, g.at[ty], g.at[ty], x_dev[1])
    a1_send(4, g.at[ty], g.at[ty], x_dev[3])
    p1[2].wait_recv()
    p2_block(2)
    lo = pl.ds(0, HALF)
    hi = pl.ds(HALF, HALF)
    a1[1].wait_recv()
    t_in = ((x + 3) % 4) * 2 + yl
    a1_send(5, g.at[t_in, :, lo], g.at[t_in, :, lo], x_dev[1])
    a1[2].wait_recv()
    t_in = ((x + 1) % 4) * 2 + yl
    a1_send(6, g.at[t_in, :, hi], g.at[t_in, :, hi], x_dev[3])
    for o in (0, 1):
        for p in range(3):
            p2_forward(p, o)
    a1[3].wait_recv()
    t_in = ((x + 3) % 4) * 2 + 1 - yl
    a1_send(7, g.at[t_in, :, lo], g.at[t_in, :, lo], x_dev[1])
    a1[4].wait_recv()
    t_in = ((x + 1) % 4) * 2 + 1 - yl
    a1_send(8, g.at[t_in, :, hi], g.at[t_in, :, hi], x_dev[3])
    for p in range(3):
        p2_forward(p, 3)

    g_cp.wait()
    w_cp.wait()
    for i in (5, 6, 7, 8):
        a1[i].wait_recv()
    gatt = dot(g[...].reshape(HD, D), w[...], NT).astype(BF16)
    for hh in range(4):
        gs[hh] = gatt[:, hh * HD : (hh + 1) * HD]
    gt = {}
    for o in (1, 3, 2):
        gt[o] = send(gs.at[(h + o) % 4], gb.at[h], gts.at[o - 1], gtr.at[o - 1], heads_dev[o])
    gb[h] = gs[h]

    for p in range(3):
        p2_forward(p, 2)
    q_cp.wait()
    for o in (1, 3, 2):
        p1q[o].wait_recv()
    for o in (0, 1, 3, 2):
        for p in (3, 4, 5, 6):
            p2[p, o].wait_recv()

    TK = 256
    col_max = [None] * 4
    for j in range(4):
        rows = 512 - HD * j
        q = qb[pl.ds(j, 4 - j)].reshape(rows, HD)

        def score_tile(kt, m, j=j, rows=rows, q=q):
            keys = kvb[0, j, pl.ds(kt * 2, 2)].reshape(TK, HD)
            s = dot(keys, q, NT) * factor
            key_pos = kt * TK + lax.broadcasted_iota(jnp.int32, (TK, HD), 0)
            row_pos = k * HD + lax.broadcasted_iota(jnp.int32, (TK, HD), 1)
            first = jnp.where(key_pos <= row_pos, s[:, :HD], -jnp.inf)
            s = first if rows == HD else jnp.concatenate([first, s[:, HD:]], axis=1)
            st[j, pl.ds(kt * TK, TK), HD * j :] = s
            return jnp.maximum(m, jnp.max(s, axis=0, keepdims=True))

        m = lax.fori_loop(0, 1024 // TK, score_tile, jnp.full((1, rows), -jnp.inf, F32))
        for s in range(j, 4):
            part = m[:, (s - j) * HD : (s - j + 1) * HD]
            col_max[s] = part if col_max[s] is None else jnp.maximum(col_max[s], part)
    m_all = jnp.concatenate(col_max, axis=1)
    total = [None] * 4
    for j in range(4):
        rows = 512 - HD * j
        mj = m_all[:, HD * j :]

        def exp_tile(kt, acc, j=j, mj=mj):
            p = jnp.exp(st[j, pl.ds(kt * TK, TK), HD * j :] - mj)
            st[j, pl.ds(kt * TK, TK), HD * j :] = p
            return acc + jnp.sum(p, axis=0, keepdims=True)

        acc = lax.fori_loop(0, 1024 // TK, exp_tile, jnp.zeros((1, rows), F32))
        for s in range(j, 4):
            part = acc[:, (s - j) * HD : (s - j + 1) * HD]
            total[s] = part if total[s] is None else total[s] + part
    inv = 1.0 / jnp.concatenate(total, axis=1)
    for j in range(4):
        rows = 512 - HD * j
        inv_j = inv[:, HD * j :]

        def norm_tile(kt, carry, j=j, inv_j=inv_j):
            p = st[j, pl.ds(kt * TK, TK), HD * j :] * inv_j
            st[j, pl.ds(kt * TK, TK), HD * j :] = p
            wl[j, pl.ds(kt * TK, TK), HD * j :] = p.astype(BF16)
            return carry

        lax.fori_loop(0, 1024 // TK, norm_tile, 0)
        vals = kvb[1, j].reshape(1024, HD)
        o_t = dot(vals, wl[j, :, HD * j :], TN)
        if j == 0:
            ot[...] = o_t
        else:
            ot[:, HD * j :] += o_t
    o_low = ot[...].astype(BF16).astype(F32)
    asend[...] = o_low.T.astype(BF16).reshape(4, HD, HD)
    at = {}
    for o in (1, 3, 2):
        at[o] = send(asend.at[(h + o) % 4], ah.at[h], ats.at[o - 1], atr.at[o - 1], heads_dev[o])
    ah[h] = asend[h]

    for o in (1, 3, 2):
        gt[o].wait_recv()
    g_t = gb[...].reshape(512, HD).astype(F32).T
    delta = jnp.sum(g_t * o_low, axis=0, keepdims=True)
    c1 = {}
    c2 = {}
    local_or_remote = []

    def home_send(src, local, remote, ssem, rsem, j):
        @pl.when(h != j)
        def _():
            pltpu.make_async_remote_copy(
                src_ref=src, dst_ref=remote, send_sem=ssem, recv_sem=rsem,
                device_id=(8 * j + k, tp), device_id_type=MESH,
            ).start()

        @pl.when(h == j)
        def _():
            local[...] = src[...]

        local_or_remote.append((src, remote, ssem, rsem, j))

    def backward(j):
        rows = 512 - HD * j
        q = qb[pl.ds(j, 4 - j)].reshape(rows, HD)
        ga = gb[pl.ds(j, 4 - j)].reshape(rows, HD)
        delta_j = delta[:, HD * j :]

        def tile(kt, carry):
            sl = pl.ds(kt * TK, TK)
            vals = kvb[1, j, pl.ds(kt * 2, 2)].reshape(TK, HD)
            dp = dot(vals, ga, NT)
            ds = (st[j, sl, HD * j :] * (dp - delta_j) * factor).astype(BF16)
            dsb[sl, HD * j :] = ds
            dkv[j, 0, pl.ds(kt * 2, 2)] = dot(ds, q, NN).reshape(2, HD, HD)
            dkv[j, 1, pl.ds(kt * 2, 2)] = dot(wl[j, sl, HD * j :], ga, NN).reshape(2, HD, HD)
            return carry

        lax.fori_loop(0, 1024 // TK, tile, 0)
        keys = kvb[0, j].reshape(1024, HD)
        dq_t = dot(keys, dsb[:, HD * j :], TN)
        if j == 0:
            dqt[...] = dq_t
        else:
            dqt[:, HD * j :] += dq_t
        for mm in range(4):
            for kv in range(2):
                sb1[j, mm, kv] = dkv[j, kv, mm * 2 + 1 - c].astype(BF16)
        c1[j] = send(sb1.at[j], rb1.at[j], c1s.at[j], c1r.at[j], core_dev)
        sbq[j] = dqt[:, HD * j : HD * (j + 1)].T.astype(BF16)
        home_send(sbq.at[j], hq.at[h], hq.at[h], dqs.at[j], dqr.at[h], j)

    def chip_sum(j):
        c1[j].wait_recv()
        for p in range(3):
            mp = group_chip[p]
            for kv in range(2):
                sb2[j, p, kv] = (dkv[j, kv, mp * 2 + c] + rb1[j, mp, kv].astype(F32)).astype(BF16)
            c2[j, p] = send(sb2.at[j, p], rb2.at[j, p], c2s.at[j, p], c2r.at[j, p], group[p])

    def finish(j):
        for p in range(3):
            c2[j, p].wait_recv()
        for kv in range(2):
            v = dkv[j, kv, k] + rb1[j, chip, kv].astype(F32)
            for p in range(3):
                v = v + rb2[j, p, kv].astype(F32)
            sb3[j, kv] = v.astype(BF16)
        home_send(sb3.at[j], hb.at[h], hb.at[h], c3s.at[j], c3r.at[h], j)

    backward(0)

    for o in (1, 3, 2):
        at[o].wait_recv()
    att = jnp.concatenate([ah[i] for i in range(4)], axis=1)
    TN_COLS = 1024

    def project(n, carry):
        cols = pl.ds(pl.multiple_of(n * TN_COLS, TN_COLS), TN_COLS)
        r = dot(att, w[:, cols], NN).reshape(4, 2, 16, TN_COLS)
        mf[:, :, :, cols] = r
        mb[:, :, :, cols] = r.astype(BF16)
        return carry

    lax.fori_loop(0, CA // TN_COLS, project, 0)
    ma = send(mb.at[:, 1 - yl, :, pl.ds(0, CA)], ra, mas.at[0], mar.at[0], y_dev)
    lax.fori_loop(CA // TN_COLS, D // TN_COLS, project, 0)
    mbx = {}
    for d in (1, 3, 2):
        mbx[d] = send(
            mb.at[(x + d) % 4, :, :, pl.ds(CA, D - CA)], rb.at[d - 1], mbs.at[d - 1], mbr.at[d - 1], x_dev[d]
        )

    backward(1)
    chip_sum(0)
    backward(2)
    chip_sum(1)
    ma.wait_recv()
    for i in range(4):
        sa[i] = (mf[i, yl, :, :CA] + ra[i].astype(F32)).astype(BF16)
    ma2 = {}
    for d in (1, 3, 2):
        ma2[d] = send(sa.at[(x + d) % 4], ra2.at[d - 1], ma2s.at[d - 1], ma2r.at[d - 1], x_dev[d])
    backward(3)
    chip_sum(2)
    chip_sum(3)
    finish(0)
    finish(1)
    for d in (1, 3, 2):
        mbx[d].wait_recv()

    def sum_b(y):
        v = mf[x, y, :, CA:]
        for d in range(3):
            v = v + rb[d, y].astype(F32)
        return v

    sb[...] = sum_b(1 - yl).astype(BF16)
    mb2 = send(sb, rbb, mb2s.at[0], mb2r.at[0], y_dev)
    finish(2)
    finish(3)
    for d in (1, 3, 2):
        ma2[d].wait_recv()
    v = mf[x, yl, :, :CA] + ra[x].astype(F32)
    for d in range(3):
        v = v + ra2[d].astype(F32)
    mixed[:, :CA] = v
    v = sum_b(yl)
    mb2.wait_recv()
    mixed[:, CA:] = v + rbb[...].astype(F32)

    for o in (1, 2, 3):
        hh = (h + o) % 4
        pltpu.make_async_remote_copy(
            src_ref=sbq.at[0], dst_ref=hq.at[hh], send_sem=dqs.at[0], recv_sem=dqr.at[hh],
            device_id=heads_dev[o], device_id_type=MESH,
        ).wait_recv()
        pltpu.make_async_remote_copy(
            src_ref=sb3.at[0], dst_ref=hb.at[hh], send_sem=c3s.at[0], recv_sem=c3r.at[hh],
            device_id=heads_dev[o], device_id_type=MESH,
        ).wait_recv()
    for i in range(4):
        gqkv[0, i] = hq[i].astype(F32)
        for kv in range(2):
            gqkv[1 + kv, i] = hb[i, kv].astype(F32)

    for cp in sends:
        cp.wait_send()
    for src, remote, ssem, rsem, j in local_or_remote:
        @pl.when(h != j)
        def _(src=src, remote=remote, ssem=ssem, rsem=rsem, j=j):
            pltpu.make_async_remote_copy(
                src_ref=src, dst_ref=remote, send_sem=ssem, recv_sem=rsem,
                device_id=(8 * j + k, tp), device_id_type=MESH,
            ).wait_send()


def per_device(qkv, grad_out, attn_out):
    dma = pltpu.SemaphoreType.DMA
    vm = pltpu.VMEM
    scratch = [
        vm((512, D), BF16),
        vm((8, 16, D), BF16),
        vm((2, 4, 8, HD, HD), BF16),
        vm((4, HD, HD), BF16),
        vm((4, 1024, 512), F32),
        vm((4, 1024, 512), BF16),
        vm((1024, 512), BF16),
        vm((HD, 512), F32),
        vm((HD, 512), F32),
        vm((4, HD, HD), BF16),
        vm((4, HD, HD), BF16),
        vm((4, HD, HD), BF16),
        vm((4, HD, HD), BF16),
        vm((4, 2, 8, HD, HD), F32),
        vm((4, 4, 2, HD, HD), BF16),
        vm((4, 4, 2, HD, HD), BF16),
        vm((4, 3, 2, HD, HD), BF16),
        vm((4, 3, 2, HD, HD), BF16),
        vm((4, 2, HD, HD), BF16),
        vm((4, 2, HD, HD), BF16),
        vm((4, HD, HD), BF16),
        vm((4, HD, HD), BF16),
        vm((4, 2, 16, D), F32),
        vm((4, 2, 16, D), BF16),
        vm((4, 16, CA), BF16),
        vm((4, 16, CA), BF16),
        vm((3, 16, CA), BF16),
        vm((3, 2, 16, D - CA), BF16),
        vm((16, D - CA), BF16),
        vm((16, D - CA), BF16),
        dma((4,)),
        dma((2, 3)), dma((2, 3)),
        dma((7, 4)), dma((7, 4)),
        dma((9,)), dma((9,)),
        dma((3,)), dma((3,)),
        dma((3,)), dma((3,)),
        dma((4,)), dma((4,)),
        dma((4, 3)), dma((4, 3)),
        dma((4,)), dma((4,)),
        dma((4,)), dma((4,)),
        dma((1,)), dma((1,)),
        dma((3,)), dma((3,)),
        dma((3,)), dma((3,)),
        dma((1,)), dma((1,)),
    ]
    qkv_t = qkv.transpose(2, 1, 0, 3)
    mixed, gq = pl.pallas_call(
        kernel,
        out_shape=(
            jax.ShapeDtypeStruct((16, D), F32),
            jax.ShapeDtypeStruct((3, 4, HD, HD), F32),
        ),
        in_specs=[pl.BlockSpec(memory_space=pl.ANY)] * 3,
        out_specs=(pl.BlockSpec(memory_space=pltpu.VMEM), pl.BlockSpec(memory_space=pltpu.VMEM)),
        scratch_shapes=scratch,
        compiler_params=pltpu.CompilerParams(
            collective_id=0, has_side_effects=True, vmem_limit_bytes=60 * 1024 * 1024
        ),
    )(qkv_t, grad_out, attn_out)
    return mixed, gq.transpose(2, 1, 0, 3)


def solution(mesh):
    in_specs = (P("ctx", "tp", None, None), P(("ctx", "tp"), None), P("tp", None))
    out_specs = (P(("ctx", "tp"), None), P("ctx", "tp", None, None))
    return jax.shard_map(
        per_device, mesh=mesh, in_specs=in_specs, out_specs=out_specs, check_vma=False
    )
```

```python
import functools
import math

import jax
import jax.numpy as jnp
from jax import lax
from jax.experimental import pallas as pl
from jax.experimental.pallas import tpu as pltpu
from jax.sharding import PartitionSpec as P

HD = 128
MESH = pl.DeviceIdType.MESH
F32 = jnp.float32
BF16 = jnp.bfloat16
D = 8192
HALF = D // 2
PIECES = 4
PC = D // PIECES
PH = PC // 2
NT = (((1,), (1,)), ((), ()))
TN = (((0,), (0,)), ((), ()))
NN = (((1,), (0,)), ((), ()))


def dot(a, b, dims):
    return lax.dot_general(a, b, dims, preferred_element_type=F32)


def kernel(
    qkv, go, wo,
    mixed, dq_out, dkv_out,
    raw, wide, qkvt, w, g, kvb, qb, st, wl, dsb, ot, dqt, gs, gb, asend, ah,
    dkv, sb1, rb1, sb2, rb2, sb3, hb, sbq, hq,
    mf, mb, r1l, r1h, accl, acch, rx, sy, ry, mo,
    lsem, ssem, p1r, p2r, p2c, a1r, gtr, atr, c1r, c2r, c3r, dqr, mr, osem,
):
    ctx = lax.axis_index("ctx")
    tp = lax.axis_index("tp")
    h = ctx // 8
    k = ctx % 8
    zb = k // 4
    yh = (k // 2) % 2
    c = k % 2
    x = tp // 2
    yl = tp % 2
    chip = k // 2
    factor = 1.0 / math.sqrt(HD)

    heads_dev = {o: (((h + o) % 4) * 8 + k, tp) for o in (1, 2, 3)}
    core_dev = (ctx + 1 - 2 * c, tp)
    group = [
        (ctx + 4 - 8 * zb, tp),
        (ctx + 2 - 4 * yh, tp),
        (ctx + 6 - 8 * zb - 4 * yh, tp),
    ]
    group_chip = [chip + 2 - 4 * zb, chip + 1 - 2 * yh, 3 - chip]
    x_dev = {d: (ctx, ((x + d) % 4) * 2 + yl) for d in (1, 2, 3)}
    y_dev = (ctx, x * 2 + 1 - yl)

    raw_cp = pltpu.make_async_copy(qkv, raw, lsem.at[1])
    raw_cp.start()
    g_cp = pltpu.make_async_copy(go, g.at[tp], lsem.at[2])
    g_cp.start()
    w_cp = pltpu.make_async_copy(wo, w, lsem.at[0])
    w_cp.start()

    everyone = list(heads_dev.values()) + [core_dev] + group + list(x_dev.values()) + [y_dev]
    barrier = pltpu.get_barrier_semaphore()
    for dev in everyone:
        pl.semaphore_signal(barrier, inc=1, device_id=dev, device_id_type=MESH)
    raw_cp.wait()
    wide[...] = raw[...].astype(F32)
    for kind in (1, 0, 2):
        for hh in range(4):
            qkvt[kind, hh] = wide[pl.ds(kind * 4 + hh, HD, stride=12), :].astype(BF16)
    for kind in range(2):
        kvb[kind, h, k] = qkvt[1 + kind, h]
    qb[h] = qkvt[0, h]
    pl.semaphore_wait(barrier, len(everyone))

    def send(src, dst, rsem, dev):
        cp = pltpu.make_async_remote_copy(
            src_ref=src, dst_ref=dst, send_sem=ssem.at[0], recv_sem=rsem, device_id=dev, device_id_type=MESH
        )
        cp.start()
        return cp

    def received(ref, rsem):
        pltpu.make_async_remote_copy(
            src_ref=ref, dst_ref=ref, send_sem=ssem.at[0], recv_sem=rsem, device_id=core_dev, device_id_type=MESH
        ).wait_recv()

    def p1_send(kind, dst, o, sem):
        return send(qkvt.at[kind, (h + o) % 4], dst, p1r.at[sem], heads_dev[o])

    p2 = {}

    def p2_send(kv, role, o, member, dev):
        part = kvb.at[kv, (h + 4 - o) % 4, member]
        if dev is core_dev:
            send(part, part, p2c.at[kv], dev)
        else:
            p2[kv, role, o] = send(part, part, p2r.at[kv, role, o], dev)

    def p2_own(kv, o):
        p2_send(kv, 0, o, k, group[0])
        p2_send(kv, 1, o, k, group[1])
        p2_send(kv, 2, o, k, core_dev)

    def p2_forward(kv, o):
        first = 1 - kv
        for side in (first, 1 - first):
            p2[kv, side, o].wait_recv()
            member = group_chip[side] * 2 + c
            if side == first:
                p2_send(kv, 2, o, member, group[1 - first])
            p2_send(kv, 3, o, member, core_dev)

    def p2_last(kv, o):
        p2[kv, 2, o].wait_recv()
        p2_send(kv, 3, o, group_chip[2] * 2 + c, core_dev)

    def p2_wait(kv):
        received(kvb.at[kv, :, pl.ds(0, 4)], p2c.at[kv])

    a1 = {}

    def a1_send(i, src, dst, dev):
        a1[i] = send(src, dst, a1r.at[min(i, 5)], dev)

    lo = pl.ds(0, HALF)
    hi = pl.ds(HALF, HALF)
    ty = x * 2 + 1 - yl

    def a1_forward(i, first, other):
        a1[first].wait_recv()
        t = ((x + 3) % 4) * 2 + other
        a1_send(i, g.at[t, :, lo], g.at[t, :, lo], x_dev[1])
        a1[first + 1].wait_recv()
        t = ((x + 1) % 4) * 2 + other
        a1_send(i + 1, g.at[t, :, hi], g.at[t, :, hi], x_dev[3])

    p1k = {}
    for o in (1, 3, 2):
        p1k[o] = p1_send(1, kvb.at[0, h, k], o, o - 1)
    p2_own(0, 0)
    a1_send(0, go, g.at[tp], y_dev)
    a1_send(1, go, g.at[tp], x_dev[1])
    a1_send(2, go, g.at[tp], x_dev[3])
    for o in (1, 3):
        p1k[o].wait_recv()
        p2_own(0, o)
    p1v = {}
    for o in (1, 3, 2):
        p1v[o] = p1_send(2, kvb.at[1, h, k], o, 2 + o)
    for o in (1, 3, 2):
        p1_send(0, qb.at[h], o, 6)
    p1k[2].wait_recv()
    p2_own(0, 2)
    p2_own(1, 0)
    a1[0].wait_recv()
    a1_send(3, g.at[ty], g.at[ty], x_dev[1])
    a1_send(4, g.at[ty], g.at[ty], x_dev[3])
    a1_forward(5, 1, yl)
    p2_forward(0, 0)
    p2_forward(0, 1)
    for o in (1, 3, 2):
        p1v[o].wait_recv()
        p2_own(1, o)
    p2_forward(0, 3)
    p2_forward(0, 2)
    p2_forward(1, 0)
    a1_forward(7, 3, 1 - yl)
    for o in (0, 1, 3, 2):
        p2_last(0, o)
    for o in (1, 3, 2):
        p2_forward(1, o)
    received(qb.at[pl.ds(0, 3)], p1r.at[6])
    p2_wait(0)

    TK = 256
    col_max = [None] * 4
    for j in range(4):
        rows = 512 - HD * j
        q = qb[pl.ds(j, 4 - j)].reshape(rows, HD)

        def score_tile(kt, m, j=j, rows=rows, q=q):
            keys = kvb[0, j, pl.ds(kt * 2, 2)].reshape(TK, HD)
            s = dot(keys, q, NT) * factor
            key_pos = kt * TK + lax.broadcasted_iota(jnp.int32, (TK, HD), 0)
            row_pos = k * HD + lax.broadcasted_iota(jnp.int32, (TK, HD), 1)
            first = jnp.where(key_pos <= row_pos, s[:, :HD], -jnp.inf)
            s = first if rows == HD else jnp.concatenate([first, s[:, HD:]], axis=1)
            st[j, pl.ds(kt * TK, TK), HD * j :] = s
            return jnp.maximum(m, jnp.max(s, axis=0, keepdims=True))

        m = lax.fori_loop(0, 1024 // TK, score_tile, jnp.full((1, rows), -jnp.inf, F32))
        for s in range(j, 4):
            part = m[:, (s - j) * HD : (s - j + 1) * HD]
            col_max[s] = part if col_max[s] is None else jnp.maximum(col_max[s], part)
    g_cp.wait()
    w_cp.wait()
    received(g.at[pl.ds(0, 2)], a1r.at[5])
    gatt = dot(g[...].reshape(HD, D), w[...], NT).astype(BF16)
    for hh in range(4):
        gs[hh] = gatt[:, hh * HD : (hh + 1) * HD]
    for o in (1, 3, 2):
        send(gs.at[(h + o) % 4], gb.at[h], gtr.at[0], heads_dev[o])
    gb[h] = gs[h]
    for o in (0, 1, 3, 2):
        p2_last(1, o)
    m_all = jnp.concatenate(col_max, axis=1)
    total = [None] * 4
    for j in range(4):
        rows = 512 - HD * j
        mj = m_all[:, HD * j :]

        def exp_tile(kt, acc, j=j, mj=mj):
            p = jnp.exp(st[j, pl.ds(kt * TK, TK), HD * j :] - mj)
            st[j, pl.ds(kt * TK, TK), HD * j :] = p
            return acc + jnp.sum(p, axis=0, keepdims=True)

        acc = lax.fori_loop(0, 1024 // TK, exp_tile, jnp.zeros((1, rows), F32))
        for s in range(j, 4):
            part = acc[:, (s - j) * HD : (s - j + 1) * HD]
            total[s] = part if total[s] is None else total[s] + part
    p2_wait(1)
    inv = 1.0 / jnp.concatenate(total, axis=1)
    for j in range(4):
        rows = 512 - HD * j
        inv_j = inv[:, HD * j :]

        def norm_tile(kt, carry, j=j, inv_j=inv_j):
            p = st[j, pl.ds(kt * TK, TK), HD * j :] * inv_j
            st[j, pl.ds(kt * TK, TK), HD * j :] = p
            wl[j, pl.ds(kt * TK, TK), HD * j :] = p.astype(BF16)
            return carry

        lax.fori_loop(0, 1024 // TK, norm_tile, 0)
        vals = kvb[1, j].reshape(1024, HD)
        o_t = dot(vals, wl[j, :, HD * j :], TN)
        if j == 0:
            ot[...] = o_t
        else:
            ot[:, HD * j :] += o_t
    o_low = ot[...].astype(BF16).astype(F32)
    asend[...] = o_low.T.astype(BF16).reshape(4, HD, HD)
    for o in (1, 3, 2):
        send(asend.at[(h + o) % 4], ah.at[h], atr.at[0], heads_dev[o])
    ah[h] = asend[h]

    received(gs.at[pl.ds(0, 3)], gtr.at[0])
    g_t = gb[...].reshape(512, HD).astype(F32).T
    delta = jnp.sum(g_t * o_low, axis=0, keepdims=True)
    c1 = {}

    def home_send(src, local, rsem, j):
        @pl.when(h != j)
        def _():
            send(src, local, rsem, (8 * j + k, tp))

        @pl.when(h == j)
        def _():
            local[...] = src[...]

    def backward(j):
        rows = 512 - HD * j
        q = qb[pl.ds(j, 4 - j)].reshape(rows, HD)
        ga = gb[pl.ds(j, 4 - j)].reshape(rows, HD)
        delta_j = delta[:, HD * j :]

        def tile(kt, carry):
            sl = pl.ds(kt * TK, TK)
            vals = kvb[1, j, pl.ds(kt * 2, 2)].reshape(TK, HD)
            dp = dot(vals, ga, NT)
            ds = (st[j, sl, HD * j :] * (dp - delta_j) * factor).astype(BF16)
            dsb[sl, HD * j :] = ds
            dkv[j, 0, pl.ds(kt * 2, 2)] = dot(ds, q, NN).reshape(2, HD, HD)
            dkv[j, 1, pl.ds(kt * 2, 2)] = dot(wl[j, sl, HD * j :], ga, NN).reshape(2, HD, HD)
            return carry

        lax.fori_loop(0, 1024 // TK, tile, 0)
        keys = kvb[0, j].reshape(1024, HD)
        dq_t = dot(keys, dsb[:, HD * j :], TN)
        if j == 0:
            dqt[...] = dq_t
        else:
            dqt[:, HD * j :] += dq_t
        for mm in range(4):
            for kv in range(2):
                sb1[j, mm, kv] = dkv[j, kv, mm * 2 + 1 - c].astype(BF16)
        c1[j] = send(sb1.at[j], rb1.at[j], c1r.at[j], core_dev)
        sbq[j] = dqt[:, HD * j : HD * (j + 1)].T.astype(BF16)
        home_send(sbq.at[j], hq.at[h], dqr.at[0], j)

    def chip_sum(j):
        c1[j].wait_recv()
        for p in range(3):
            mp = group_chip[p]
            for kv in range(2):
                sb2[j, p, kv] = (dkv[j, kv, mp * 2 + c] + rb1[j, mp, kv].astype(F32)).astype(BF16)
            send(sb2.at[j, p], rb2.at[j, p], c2r.at[j], group[p])

    def finish(j):
        received(rb2.at[j], c2r.at[j])
        for kv in range(2):
            v = dkv[j, kv, k] + rb1[j, chip, kv].astype(F32)
            for p in range(3):
                v = v + rb2[j, p, kv].astype(F32)
            sb3[j, kv] = v.astype(BF16)
        home_send(sb3.at[j], hb.at[h], c3r.at[0], j)

    backward(0)
    backward(1)
    chip_sum(0)

    received(asend.at[pl.ds(0, 3)], atr.at[0])
    att = jnp.concatenate([ah[i] for i in range(4)], axis=1)
    m_cp = {}
    xr, xo, xl = (x + 1) % 4, (x + 2) % 4, (x + 3) % 4

    def m_send(n, i, src, dst, dev):
        m_cp[n, i] = send(src, dst, mr.at[n, i], dev)

    def project(n):
        for half in range(2):
            cols = pl.ds(n * PC + half * PH, PH)
            r = dot(att, w[:, cols], NN).reshape(4, 2, 16, PH)
            mf[:, :, :, cols] = r
            mb[:, :, :, cols] = r.astype(BF16)
        left = pl.ds(n * PC, PH)
        right = pl.ds(n * PC + PH, PH)
        m_send(n, 0, mb.at[xo, :, :, left], r1l.at[n], x_dev[1])
        m_send(n, 1, mb.at[xo, :, :, right], r1h.at[n], x_dev[3])
        m_send(n, 2, mb.at[xr, :, :, right], rx.at[n, 0, :, :, pl.ds(PH, PH)], x_dev[1])
        m_send(n, 2, mb.at[xl, :, :, left], rx.at[n, 1, :, :, pl.ds(0, PH)], x_dev[3])

    def pass_on(n):
        m_cp[n, 0].wait_recv()
        accl[n] = (mf[xr, :, :, pl.ds(n * PC, PH)] + r1l[n].astype(F32)).astype(BF16)
        m_send(n, 2, accl.at[n], rx.at[n, 0, :, :, pl.ds(0, PH)], x_dev[1])
        m_cp[n, 1].wait_recv()
        acch[n] = (mf[xl, :, :, pl.ds(n * PC + PH, PH)] + r1h[n].astype(F32)).astype(BF16)
        m_send(n, 2, acch.at[n], rx.at[n, 1, :, :, pl.ds(PH, PH)], x_dev[3])

    def x_total(n, y):
        return mf[x, y, :, pl.ds(n * PC, PC)] + rx[n, 0, y].astype(F32) + rx[n, 1, y].astype(F32)

    def over_y(n):
        received(rx.at[n], mr.at[n, 2])
        sy[n] = x_total(n, 1 - yl).astype(BF16)
        m_send(n, 3, sy.at[n], ry.at[n], y_dev)

    def out(src, dst, i):
        pltpu.make_async_copy(src, dst, osem.at[i]).start()

    def last_sum(n):
        v = x_total(n, yl)
        m_cp[n, 3].wait_recv()
        cols = pl.ds(n * PC, PC)
        mo[:, cols] = v + ry[n].astype(F32)
        out(mo.at[:, cols], mixed.at[:, cols], 0)

    for n in range(PIECES):
        project(n)
    backward(2)
    chip_sum(1)
    pass_on(0)
    backward(3)
    chip_sum(2)
    pass_on(1)
    chip_sum(3)
    finish(0)
    pass_on(2)
    finish(1)
    pass_on(3)
    over_y(0)
    finish(2)
    over_y(1)
    finish(3)
    over_y(2)
    over_y(3)
    for n in range(PIECES):
        last_sum(n)

    received(sbq.at[pl.ds(0, 3)], dqr.at[0])
    out(hq, dq_out, 1)
    received(sb3.at[pl.ds(0, 3)], c3r.at[0])
    out(hb, dkv_out, 2)

    everything = w.at[pl.ds(0, 496)]
    pltpu.make_async_remote_copy(
        src_ref=everything, dst_ref=everything, send_sem=ssem.at[0], recv_sem=p1r.at[0],
        device_id=core_dev, device_id_type=MESH,
    ).wait_send()
    pltpu.make_async_copy(mo, mixed, osem.at[0]).wait()
    pltpu.make_async_copy(hq, dq_out, osem.at[1]).wait()
    pltpu.make_async_copy(hb, dkv_out, osem.at[2]).wait()


def finish_kernel(mixed_in, dq, dkv, mixed, rows_out, rows, sem):
    copies = [pltpu.make_async_copy(mixed_in, mixed, sem.at[0])]
    copies[0].start()
    n = 32
    for part in range(HD // n):
        pos = pl.ds(part * n, n)
        for i in range(4):
            for kind in range(3):
                v = dq[i, pos] if kind == 0 else dkv[i, kind - 1, pos]
                rows[pl.ds(part * n * 12 + kind * 4 + i, n, stride=12), :] = v.astype(F32)
        span = pl.ds(part * n * 12, n * 12)
        copies.append(pltpu.make_async_copy(rows.at[span], rows_out.at[span], sem.at[1 + part]))
        copies[-1].start()
    for cp in copies:
        cp.wait()


def per_device(qkv, grad_out, attn_out):
    dma = pltpu.SemaphoreType.DMA
    vm = pltpu.VMEM
    scratch = [
        vm((1536, HD), BF16),
        vm((1536, HD), F32),
        vm((3, 4, HD, HD), BF16),
        vm((512, D), BF16),
        vm((8, 16, D), BF16),
        vm((2, 4, 8, HD, HD), BF16),
        vm((4, HD, HD), BF16),
        vm((4, 1024, 512), F32),
        vm((4, 1024, 512), BF16),
        vm((1024, 512), BF16),
        vm((HD, 512), F32),
        vm((HD, 512), F32),
        vm((4, HD, HD), BF16),
        vm((4, HD, HD), BF16),
        vm((4, HD, HD), BF16),
        vm((4, HD, HD), BF16),
        vm((4, 2, 8, HD, HD), F32),
        vm((4, 4, 2, HD, HD), BF16),
        vm((4, 4, 2, HD, HD), BF16),
        vm((4, 3, 2, HD, HD), BF16),
        vm((4, 3, 2, HD, HD), BF16),
        vm((4, 2, HD, HD), BF16),
        vm((4, 2, HD, HD), BF16),
        vm((4, HD, HD), BF16),
        vm((4, HD, HD), BF16),
        vm((4, 2, 16, D), F32),
        vm((4, 2, 16, D), BF16),
        vm((PIECES, 2, 16, PH), BF16),
        vm((PIECES, 2, 16, PH), BF16),
        vm((PIECES, 2, 16, PH), BF16),
        vm((PIECES, 2, 16, PH), BF16),
        vm((PIECES, 2, 2, 16, PC), BF16),
        vm((PIECES, 16, PC), BF16),
        vm((PIECES, 16, PC), BF16),
        vm((16, D), F32),
        dma((3,)),
        dma((1,)),
        dma((7,)),
        dma((2, 3, 4)), dma((2,)),
        dma((6,)),
        dma((1,)), dma((1,)),
        dma((4,)), dma((4,)),
        dma((1,)), dma((1,)),
        dma((PIECES, 4)),
        dma((3,)),
    ]
    rows = qkv.transpose(0, 2, 1, 3).reshape(1536, HD)
    mixed, dq, dkv = pl.pallas_call(
        kernel,
        out_shape=(
            jax.ShapeDtypeStruct((16, D), F32),
            jax.ShapeDtypeStruct((4, HD, HD), BF16),
            jax.ShapeDtypeStruct((4, 2, HD, HD), BF16),
        ),
        in_specs=[pl.BlockSpec(memory_space=pl.ANY)] * 3,
        out_specs=[pl.BlockSpec(memory_space=pl.ANY)] * 3,
        scratch_shapes=scratch,
        compiler_params=pltpu.CompilerParams(
            collective_id=0, has_side_effects=True, vmem_limit_bytes=60 * 1024 * 1024
        ),
    )(rows, grad_out, attn_out)
    mixed, grads = pl.pallas_call(
        finish_kernel,
        out_shape=(
            jax.ShapeDtypeStruct((16, D), F32),
            jax.ShapeDtypeStruct((1536, HD), F32),
        ),
        in_specs=[pl.BlockSpec(memory_space=pltpu.VMEM)] * 3,
        out_specs=[pl.BlockSpec(memory_space=pl.ANY)] * 2,
        scratch_shapes=[pltpu.VMEM((1536, HD), F32), pltpu.SemaphoreType.DMA((5,))],
    )(mixed, dq, dkv)
    return mixed, grads.reshape(HD, 3, 4, HD).transpose(0, 2, 1, 3)


def solution(mesh):
    in_specs = (P("ctx", "tp", None, None), P(("ctx", "tp"), None), P("tp", None))
    out_specs = (P(("ctx", "tp"), None), P("ctx", "tp", None, None))
    return jax.shard_map(
        per_device, mesh=mesh, in_specs=in_specs, out_specs=out_specs, check_vma=False
    )
```

```python
import functools
import math

import jax
import jax.numpy as jnp
from jax import lax
from jax.experimental import pallas as pl
from jax.experimental.pallas import tpu as pltpu
from jax.sharding import PartitionSpec as P

HD = 128
MESH = pl.DeviceIdType.MESH
F32 = jnp.float32
BF16 = jnp.bfloat16
D = 8192
HALF = D // 2
PIECES = 4
PC = D // PIECES
PH = PC // 2
NT = (((1,), (1,)), ((), ()))
TN = (((0,), (0,)), ((), ()))
NN = (((1,), (0,)), ((), ()))


def dot(a, b, dims):
    return lax.dot_general(a, b, dims, preferred_element_type=F32)


def kernel(
    qkv, go, wo,
    mixed, dq_out, dkv_out,
    raw, wide, qkvt, w, g, kvb, qb, st, wl, dsb, ot, dqt, gs, gb, asend, ah,
    dkv, sb1, rb1, s2a, r2a, s2b, r2b, sb3, hb, sbq, hq,
    mf, mb, r1l, r1h, accl, acch, rx, sy, ry, ra, sa, r1a, acca, rxa, mo,
    lsem, ssem, p1r, p2r, p2c, a1r, gtr, atr, c1r, c2r, c3r, dqr, mr, osem,
):
    ctx = lax.axis_index("ctx")
    tp = lax.axis_index("tp")
    h = ctx // 8
    k = ctx % 8
    zb = k // 4
    yh = (k // 2) % 2
    c = k % 2
    x = tp // 2
    yl = tp % 2
    chip = k // 2
    factor = 1.0 / math.sqrt(HD)

    heads_dev = {o: (((h + o) % 4) * 8 + k, tp) for o in (1, 2, 3)}
    core_dev = (ctx + 1 - 2 * c, tp)
    group = [
        (ctx + 4 - 8 * zb, tp),
        (ctx + 2 - 4 * yh, tp),
        (ctx + 6 - 8 * zb - 4 * yh, tp),
    ]
    group_chip = [chip + 2 - 4 * zb, chip + 1 - 2 * yh, 3 - chip]
    x_dev = {d: (ctx, ((x + d) % 4) * 2 + yl) for d in (1, 2, 3)}
    y_dev = (ctx, x * 2 + 1 - yl)

    raw_cp = pltpu.make_async_copy(qkv, raw, lsem.at[1])
    raw_cp.start()
    g_cp = pltpu.make_async_copy(go, g.at[tp], lsem.at[2])
    g_cp.start()
    w_cp = pltpu.make_async_copy(wo, w, lsem.at[0])
    w_cp.start()

    everyone = list(heads_dev.values()) + [core_dev] + group + list(x_dev.values()) + [y_dev]
    barrier = pltpu.get_barrier_semaphore()
    for dev in everyone:
        pl.semaphore_signal(barrier, inc=1, device_id=dev, device_id_type=MESH)
    raw_cp.wait()
    wide[...] = raw[...].astype(F32)
    for kind in (1, 0, 2):
        for hh in range(4):
            qkvt[kind, hh] = wide[pl.ds(kind * 4 + hh, HD, stride=12), :].astype(BF16)
    for kind in range(2):
        kvb[kind, h, k] = qkvt[1 + kind, h]
    qb[h] = qkvt[0, h]
    pl.semaphore_wait(barrier, len(everyone))

    def send(src, dst, rsem, dev):
        cp = pltpu.make_async_remote_copy(
            src_ref=src, dst_ref=dst, send_sem=ssem.at[0], recv_sem=rsem, device_id=dev, device_id_type=MESH
        )
        cp.start()
        return cp

    def received(ref, rsem):
        pltpu.make_async_remote_copy(
            src_ref=ref, dst_ref=ref, send_sem=ssem.at[0], recv_sem=rsem, device_id=core_dev, device_id_type=MESH
        ).wait_recv()

    def p1_send(kind, dst, o, sem):
        return send(qkvt.at[kind, (h + o) % 4], dst, p1r.at[sem], heads_dev[o])

    p2 = {}

    def p2_send(kv, role, o, member, dev):
        part = kvb.at[kv, (h + 4 - o) % 4, member]
        if dev is core_dev:
            send(part, part, p2c.at[kv], dev)
        else:
            p2[kv, role, o] = send(part, part, p2r.at[kv, role, o], dev)

    def p2_own(kv, o):
        p2_send(kv, 0, o, k, group[0])
        p2_send(kv, 1, o, k, group[1])
        p2_send(kv, 2, o, k, core_dev)

    def p2_forward(kv, o):
        first = 1 if kv == 0 and o < 2 else 0
        for side in (first, 1 - first):
            p2[kv, side, o].wait_recv()
            member = group_chip[side] * 2 + c
            if side == first:
                p2_send(kv, 2, o, member, group[1 - first])
            p2_send(kv, 3, o, member, core_dev)

    def p2_last(kv, o):
        p2[kv, 2, o].wait_recv()
        p2_send(kv, 3, o, group_chip[2] * 2 + c, core_dev)

    def p2_wait(kv):
        received(kvb.at[kv, :, pl.ds(0, 4)], p2c.at[kv])

    lo = pl.ds(0, HALF)
    hi = pl.ds(HALF, HALF)
    ty = x * 2 + 1 - yl

    def a1_send(src, t, half, sem, dev):
        return send(src.at[:, half], g.at[t, :, half], a1r.at[sem], dev)

    def a1_forward(i, other):
        received(g.at[0, :, lo], a1r.at[i])
        t = ((x + 3) % 4) * 2 + other
        a1_send(g.at[t], t, lo, 6, x_dev[1])
        received(g.at[0, :, hi], a1r.at[i + 1])
        t = ((x + 1) % 4) * 2 + other
        a1_send(g.at[t], t, hi, 6, x_dev[3])

    p1k = {}
    for o in (1, 3, 2):
        p1k[o] = p1_send(1, kvb.at[0, h, k], o, o - 1)
    a1_send(go, tp, lo, 2, x_dev[1])
    a1_send(go, tp, hi, 3, x_dev[3])
    a1_send(go, tp, lo, 0, y_dev)
    a1_send(go, tp, hi, 1, y_dev)
    a1_send(go, tp, hi, 6, x_dev[1])
    a1_send(go, tp, lo, 6, x_dev[3])
    p2_own(0, 0)
    for o in (1, 3):
        p1k[o].wait_recv()
        p2_own(0, o)
    p1v = {}
    for o in (1, 3, 2):
        p1v[o] = p1_send(2, kvb.at[1, h, k], o, 2 + o)
    a1_forward(2, yl)
    received(g.at[0, :, lo], a1r.at[0])
    a1_send(g.at[ty], ty, lo, 4, x_dev[1])
    p1k[2].wait_recv()
    p2_own(0, 2)
    for o in (1, 3, 2):
        p1_send(0, qb.at[h], o, 6)
    received(g.at[0, :, hi], a1r.at[1])
    a1_send(g.at[ty], ty, hi, 5, x_dev[3])
    a1_send(g.at[ty], ty, hi, 6, x_dev[1])
    a1_send(g.at[ty], ty, lo, 6, x_dev[3])
    for o in (0, 1, 3, 2):
        p2_forward(0, o)
    p2_own(1, 0)
    for o in (1, 3, 2):
        p1v[o].wait_recv()
        p2_own(1, o)
    a1_forward(4, 1 - yl)
    p2_forward(1, 0)
    for o in (0, 1, 3, 2):
        p2_last(0, o)
    for o in (1, 3, 2):
        p2_forward(1, o)
    received(qb.at[pl.ds(0, 3)], p1r.at[6])
    p2_wait(0)

    col_max = [None] * 4
    key_pos = lax.broadcasted_iota(jnp.int32, (1024, HD), 0)
    row_pos = k * HD + lax.broadcasted_iota(jnp.int32, (1024, HD), 1)
    for j in range(4):
        rows = 512 - HD * j
        s = dot(kvb[0, j].reshape(1024, HD), qb[pl.ds(j, 4 - j)].reshape(rows, HD), NT) * factor
        first = jnp.where(key_pos <= row_pos, s[:, :HD], -jnp.inf)
        s = first if rows == HD else jnp.concatenate([first, s[:, HD:]], axis=1)
        st[j, :, HD * j :] = s
        m = jnp.max(s, axis=0, keepdims=True)
        for i in range(j, 4):
            part = m[:, (i - j) * HD : (i - j + 1) * HD]
            col_max[i] = part if col_max[i] is None else jnp.maximum(col_max[i], part)
    m_all = jnp.concatenate(col_max, axis=1)
    total = [None] * 4
    for j in range(4):
        p = jnp.exp(st[j, :, HD * j :] - m_all[:, HD * j :])
        st[j, :, HD * j :] = p
        m = jnp.sum(p, axis=0, keepdims=True)
        for i in range(j, 4):
            part = m[:, (i - j) * HD : (i - j + 1) * HD]
            total[i] = part if total[i] is None else total[i] + part
    inv = 1.0 / jnp.concatenate(total, axis=1)
    g_cp.wait()
    w_cp.wait()
    received(g.at[pl.ds(0, 4)], a1r.at[6])
    gatt = dot(g[:, :, :HALF].reshape(HD, HALF), w[:, :HALF], NT)
    for o in (0, 1, 3, 2):
        p2_last(1, o)
    gatt = (gatt + dot(g[:, :, HALF:].reshape(HD, HALF), w[:, HALF:], NT)).astype(BF16)
    for hh in range(4):
        gs[hh] = gatt[:, hh * HD : (hh + 1) * HD]
    for o in (1, 3, 2):
        send(gs.at[(h + o) % 4], gb.at[h], gtr.at[0], heads_dev[o])
    gb[h] = gs[h]
    p2_wait(1)
    for j in range(4):
        p = st[j, :, HD * j :] * inv[:, HD * j :]
        st[j, :, HD * j :] = p
        p_low = p.astype(BF16)
        wl[j, :, HD * j :] = p_low
        o_t = dot(kvb[1, j].reshape(1024, HD), p_low, TN)
        if j == 0:
            ot[...] = o_t
        else:
            ot[:, HD * j :] += o_t
    o_low = ot[...].astype(BF16).astype(F32)
    asend[...] = o_low.T.astype(BF16).reshape(4, HD, HD)
    for o in (1, 3, 2):
        send(asend.at[(h + o) % 4], ah.at[h], atr.at[0], heads_dev[o])
    ah[h] = asend[h]

    c1 = {}

    def home_send(src, local, rsem, j):
        @pl.when(h != j)
        def _():
            send(src, local, rsem, (8 * j + k, tp))

        @pl.when(h == j)
        def _():
            local[...] = src[...]

    def backward(j):
        rows = 512 - HD * j
        q = qb[pl.ds(j, 4 - j)].reshape(rows, HD)
        ga = gb[pl.ds(j, 4 - j)].reshape(rows, HD)
        delta_j = delta[:, HD * j :]

        dp = dot(kvb[1, j].reshape(1024, HD), ga, NT)
        ds = (st[j, :, HD * j :] * (dp - delta_j) * factor).astype(BF16)
        dsb[:, HD * j :] = ds
        dkv[j, 0] = dot(ds, q, NN).reshape(8, HD, HD)
        dkv[j, 1] = dot(wl[j, :, HD * j :], ga, NN).reshape(8, HD, HD)
        keys = kvb[0, j].reshape(1024, HD)
        dq_t = dot(keys, dsb[:, HD * j :], TN)
        if j == 0:
            dqt[...] = dq_t
        else:
            dqt[:, HD * j :] += dq_t
        for mm in range(4):
            for kv in range(2):
                sb1[j, mm, kv] = dkv[j, kv, mm * 2 + 1 - c].astype(BF16)
        c1[j] = send(sb1.at[j], rb1.at[j], c1r.at[j], core_dev)
        sbq[j] = dqt[:, HD * j : HD * (j + 1)].T.astype(BF16)
        home_send(sbq.at[j], hq.at[h], dqr.at[0], j)

    def of_chip(j, kv, mp):
        return dkv[j, kv, mp * 2 + c] + rb1[j, mp, kv].astype(F32)

    def chip_sum(j):
        c1[j].wait_recv()
        for kv in range(2):
            s2a[j, kv, 0] = of_chip(j, kv, group_chip[kv]).astype(BF16)
            s2a[j, kv, 1] = of_chip(j, kv, group_chip[2]).astype(BF16)
            send(s2a.at[j, kv], r2a.at[j, kv], c2r.at[0, j], group[kv])

    def relay(j):
        received(r2a.at[j], c2r.at[0, j])
        for kv in range(2):
            s2b[j, kv] = (of_chip(j, kv, group_chip[1 - kv]) + r2a[j, kv, 1].astype(F32)).astype(BF16)
            send(s2b.at[j, kv], r2b.at[j, kv], c2r.at[1, j], group[1 - kv])

    def finish(j):
        received(r2b.at[j], c2r.at[1, j])
        for kv in range(2):
            v = of_chip(j, kv, chip) + r2a[j, kv, 0].astype(F32) + r2b[j, kv].astype(F32)
            sb3[j, kv] = v.astype(BF16)
        home_send(sb3.at[j], hb.at[h], c3r.at[0], j)

    m_cp = {}
    xr, xo, xl = (x + 1) % 4, (x + 2) % 4, (x + 3) % 4

    def m_send(n, i, src, dst, dev):
        m_cp[n, i] = send(src, dst, mr.at[n, i], dev)

    def project(n):
        for half in range(2):
            cols = pl.ds(n * PC + half * PH, PH)
            r = dot(att, w[:, cols], NN).reshape(4, 2, 16, PH)
            mf[:, :, :, cols] = r
            mb[:, :, :, cols] = r.astype(BF16)

    def first_hop(n):
        left = pl.ds(n * PC, PH)
        right = pl.ds(n * PC + PH, PH)
        m_send(n, 0, mb.at[xo, :, :, left], r1l.at[n], x_dev[1])
        m_send(n, 1, mb.at[xo, :, :, right], r1h.at[n], x_dev[3])

    def direct(n):
        left = pl.ds(n * PC, PH)
        right = pl.ds(n * PC + PH, PH)
        m_send(n, 2, mb.at[xr, :, :, right], rx.at[n, 0, :, :, pl.ds(PH, PH)], x_dev[1])
        m_send(n, 2, mb.at[xl, :, :, left], rx.at[n, 1, :, :, pl.ds(0, PH)], x_dev[3])

    def pass_on(n):
        m_cp[n, 0].wait_recv()
        accl[n] = (mf[xr, :, :, pl.ds(n * PC, PH)] + r1l[n].astype(F32)).astype(BF16)
        m_send(n, 2, accl.at[n], rx.at[n, 0, :, :, pl.ds(0, PH)], x_dev[1])
        m_cp[n, 1].wait_recv()
        acch[n] = (mf[xl, :, :, pl.ds(n * PC + PH, PH)] + r1h[n].astype(F32)).astype(BF16)
        m_send(n, 2, acch.at[n], rx.at[n, 1, :, :, pl.ds(PH, PH)], x_dev[3])

    last = PIECES - 1
    cols_a = pl.ds(last * PC, PC)

    def a_over_y():
        m_send(last, 3, mb.at[:, 1 - yl, :, cols_a], ra, y_dev)

    def a_first_hop():
        m_cp[last, 3].wait_recv()
        for i in range(4):
            v = mf[i, yl, :, cols_a] + ra[i].astype(F32)
            mf[i, yl, :, cols_a] = v
            sa[i] = v.astype(BF16)
        m_send(last, 0, sa.at[xo, :, pl.ds(0, PH)], r1a.at[0], x_dev[1])
        m_send(last, 1, sa.at[xo, :, pl.ds(PH, PH)], r1a.at[1], x_dev[3])
        m_send(last, 2, sa.at[xr, :, pl.ds(PH, PH)], rxa.at[0, :, pl.ds(PH, PH)], x_dev[1])
        m_send(last, 2, sa.at[xl, :, pl.ds(0, PH)], rxa.at[1, :, pl.ds(0, PH)], x_dev[3])

    def a_pass_on():
        m_cp[last, 0].wait_recv()
        acca[0] = (mf[xr, yl, :, pl.ds(last * PC, PH)] + r1a[0].astype(F32)).astype(BF16)
        m_send(last, 2, acca.at[0], rxa.at[0, :, pl.ds(0, PH)], x_dev[1])
        m_cp[last, 1].wait_recv()
        acca[1] = (mf[xl, yl, :, pl.ds(last * PC + PH, PH)] + r1a[1].astype(F32)).astype(BF16)
        m_send(last, 2, acca.at[1], rxa.at[1, :, pl.ds(PH, PH)], x_dev[3])

    def a_last_sum():
        received(rxa, mr.at[last, 2])
        mo[:, cols_a] = mf[x, yl, :, cols_a] + rxa[0].astype(F32) + rxa[1].astype(F32)
        out(mo.at[:, cols_a], mixed.at[:, cols_a], 0)

    def x_total(n, y):
        return mf[x, y, :, pl.ds(n * PC, PC)] + rx[n, 0, y].astype(F32) + rx[n, 1, y].astype(F32)

    def over_y(n):
        received(rx.at[n], mr.at[n, 2])
        sy[n] = x_total(n, 1 - yl).astype(BF16)
        m_send(n, 3, sy.at[n], ry.at[n], y_dev)

    def out(src, dst, i):
        pltpu.make_async_copy(src, dst, osem.at[i]).start()

    def last_sum(n):
        v = x_total(n, yl)
        m_cp[n, 3].wait_recv()
        cols = pl.ds(n * PC, PC)
        mo[:, cols] = v + ry[n].astype(F32)
        out(mo.at[:, cols], mixed.at[:, cols], 0)

    received(gs.at[pl.ds(0, 3)], gtr.at[0])
    g_t = gb[...].reshape(512, HD).astype(F32).T
    delta = jnp.sum(g_t * o_low, axis=0, keepdims=True)
    backward(0)
    received(asend.at[pl.ds(0, 3)], atr.at[0])
    att = jnp.concatenate([ah[i] for i in range(4)], axis=1)
    project(last)
    a_over_y()
    for n in range(last):
        project(n)
        first_hop(n)
    direct(0)
    direct(1)
    backward(1)
    chip_sum(0)
    pass_on(0)
    direct(2)
    backward(2)
    chip_sum(1)
    pass_on(1)
    backward(3)
    chip_sum(2)
    relay(0)
    pass_on(2)
    chip_sum(3)
    relay(1)
    a_first_hop()
    relay(2)
    over_y(0)
    relay(3)
    finish(0)
    a_pass_on()
    finish(1)
    over_y(1)
    finish(2)
    finish(3)
    over_y(2)
    for n in range(last):
        last_sum(n)
    a_last_sum()
    received(sbq.at[pl.ds(0, 3)], dqr.at[0])
    out(hq, dq_out, 1)
    received(sb3.at[pl.ds(0, 3)], c3r.at[0])
    out(hb, dkv_out, 2)

    everything = w.at[pl.ds(0, 496)]
    pltpu.make_async_remote_copy(
        src_ref=everything, dst_ref=everything, send_sem=ssem.at[0], recv_sem=p1r.at[0],
        device_id=core_dev, device_id_type=MESH,
    ).wait_send()
    pltpu.make_async_copy(mo, mixed, osem.at[0]).wait()
    pltpu.make_async_copy(hq, dq_out, osem.at[1]).wait()
    pltpu.make_async_copy(hb, dkv_out, osem.at[2]).wait()


def finish_kernel(mixed_in, dq, dkv, mixed, rows_out, rows, sem):
    copies = [pltpu.make_async_copy(mixed_in, mixed, sem.at[0])]
    copies[0].start()
    n = 32
    for part in range(HD // n):
        pos = pl.ds(part * n, n)
        for i in range(4):
            for kind in range(3):
                v = dq[i, pos] if kind == 0 else dkv[i, kind - 1, pos]
                rows[pl.ds(part * n * 12 + kind * 4 + i, n, stride=12), :] = v.astype(F32)
        span = pl.ds(part * n * 12, n * 12)
        copies.append(pltpu.make_async_copy(rows.at[span], rows_out.at[span], sem.at[1 + part]))
        copies[-1].start()
    for cp in copies:
        cp.wait()


def per_device(qkv, grad_out, attn_out):
    dma = pltpu.SemaphoreType.DMA
    vm = pltpu.VMEM
    scratch = [
        vm((1536, HD), BF16),
        vm((1536, HD), F32),
        vm((3, 4, HD, HD), BF16),
        vm((512, D), BF16),
        vm((8, 16, D), BF16),
        vm((2, 4, 8, HD, HD), BF16),
        vm((4, HD, HD), BF16),
        vm((4, 1024, 512), F32),
        vm((4, 1024, 512), BF16),
        vm((1024, 512), BF16),
        vm((HD, 512), F32),
        vm((HD, 512), F32),
        vm((4, HD, HD), BF16),
        vm((4, HD, HD), BF16),
        vm((4, HD, HD), BF16),
        vm((4, HD, HD), BF16),
        vm((4, 2, 8, HD, HD), F32),
        vm((4, 4, 2, HD, HD), BF16),
        vm((4, 4, 2, HD, HD), BF16),
        vm((4, 2, 2, HD, HD), BF16),
        vm((4, 2, 2, HD, HD), BF16),
        vm((4, 2, HD, HD), BF16),
        vm((4, 2, HD, HD), BF16),
        vm((4, 2, HD, HD), BF16),
        vm((4, 2, HD, HD), BF16),
        vm((4, HD, HD), BF16),
        vm((4, HD, HD), BF16),
        vm((4, 2, 16, D), F32),
        vm((4, 2, 16, D), BF16),
        vm((PIECES - 1, 2, 16, PH), BF16),
        vm((PIECES - 1, 2, 16, PH), BF16),
        vm((PIECES - 1, 2, 16, PH), BF16),
        vm((PIECES - 1, 2, 16, PH), BF16),
        vm((PIECES - 1, 2, 2, 16, PC), BF16),
        vm((PIECES - 1, 16, PC), BF16),
        vm((PIECES - 1, 16, PC), BF16),
        vm((4, 16, PC), BF16),
        vm((4, 16, PC), BF16),
        vm((2, 16, PH), BF16),
        vm((2, 16, PH), BF16),
        vm((2, 16, PC), BF16),
        vm((16, D), F32),
        dma((3,)),
        dma((1,)),
        dma((7,)),
        dma((2, 3, 4)), dma((2,)),
        dma((7,)),
        dma((1,)), dma((1,)),
        dma((4,)), dma((2, 4)),
        dma((1,)), dma((1,)),
        dma((PIECES, 4)),
        dma((3,)),
    ]
    rows = qkv.transpose(0, 2, 1, 3).reshape(1536, HD)
    mixed, dq, dkv = pl.pallas_call(
        kernel,
        out_shape=(
            jax.ShapeDtypeStruct((16, D), F32),
            jax.ShapeDtypeStruct((4, HD, HD), BF16),
            jax.ShapeDtypeStruct((4, 2, HD, HD), BF16),
        ),
        in_specs=[pl.BlockSpec(memory_space=pl.ANY)] * 3,
        out_specs=[pl.BlockSpec(memory_space=pl.ANY)] * 3,
        scratch_shapes=scratch,
        compiler_params=pltpu.CompilerParams(
            collective_id=0, has_side_effects=True, vmem_limit_bytes=60 * 1024 * 1024
        ),
    )(rows, grad_out, attn_out)
    mixed, grads = pl.pallas_call(
        finish_kernel,
        out_shape=(
            jax.ShapeDtypeStruct((16, D), F32),
            jax.ShapeDtypeStruct((1536, HD), F32),
        ),
        in_specs=[pl.BlockSpec(memory_space=pltpu.VMEM)] * 3,
        out_specs=[pl.BlockSpec(memory_space=pl.ANY)] * 2,
        scratch_shapes=[pltpu.VMEM((1536, HD), F32), pltpu.SemaphoreType.DMA((5,))],
    )(mixed, dq, dkv)
    return mixed, grads.reshape(HD, 3, 4, HD).transpose(0, 2, 1, 3)


def solution(mesh):
    in_specs = (P("ctx", "tp", None, None), P(("ctx", "tp"), None), P("tp", None))
    out_specs = (P(("ctx", "tp"), None), P("ctx", "tp", None, None))
    return jax.shard_map(
        per_device, mesh=mesh, in_specs=in_specs, out_specs=out_specs, check_vma=False
    )
```

```python
import functools
import math

import jax
import jax.numpy as jnp
from jax import lax
from jax.experimental import pallas as pl
from jax.experimental.pallas import tpu as pltpu
from jax.sharding import PartitionSpec as P

HD = 128
MESH = pl.DeviceIdType.MESH
F32 = jnp.float32
BF16 = jnp.bfloat16
D = 8192
HALF = D // 2
PIECES = 4
PC = D // PIECES
PH = PC // 2
NT = (((1,), (1,)), ((), ()))
TN = (((0,), (0,)), ((), ()))
NN = (((1,), (0,)), ((), ()))


def dot(a, b, dims):
    return lax.dot_general(a, b, dims, preferred_element_type=F32)


def kernel(
    qkv, go, wo,
    mixed, dq_out, dkv_out,
    raw, wide, qkvt, w, g, kvb, qb, st, wl, dsb, ot, dqt, gs, gb, asend, ah,
    dkv, sb1, rb1, s2a, r2a, s2b, r2b, sb3, hb, sbq, hq,
    mf, mb, r1l, r1h, accl, acch, rx, sy, ry, ra, sa, r1a, acca, rxa, mo,
    lsem, ssem, p1r, p2r, p2c, a1r, gtr, atr, c1r, c2r, c3r, dqr, mr, osem,
):
    ctx = lax.axis_index("ctx")
    tp = lax.axis_index("tp")
    h = ctx // 8
    k = ctx % 8
    zb = k // 4
    yh = (k // 2) % 2
    c = k % 2
    x = tp // 2
    yl = tp % 2
    chip = k // 2
    factor = 1.0 / math.sqrt(HD)

    heads_dev = {o: (((h + o) % 4) * 8 + k, tp) for o in (1, 2, 3)}
    core_dev = (ctx + 1 - 2 * c, tp)
    group = [
        (ctx + 4 - 8 * zb, tp),
        (ctx + 2 - 4 * yh, tp),
        (ctx + 6 - 8 * zb - 4 * yh, tp),
    ]
    group_chip = [chip + 2 - 4 * zb, chip + 1 - 2 * yh, 3 - chip]
    x_dev = {d: (ctx, ((x + d) % 4) * 2 + yl) for d in (1, 2, 3)}
    y_dev = (ctx, x * 2 + 1 - yl)

    raw_cp = pltpu.make_async_copy(qkv, raw, lsem.at[1])
    raw_cp.start()
    g_cp = pltpu.make_async_copy(go, g.at[tp], lsem.at[2])
    g_cp.start()
    w_cp = pltpu.make_async_copy(wo, w, lsem.at[0])
    w_cp.start()

    everyone = list(heads_dev.values()) + [core_dev] + group + list(x_dev.values()) + [y_dev]
    barrier = pltpu.get_barrier_semaphore()
    for dev in everyone:
        pl.semaphore_signal(barrier, inc=1, device_id=dev, device_id_type=MESH)
    raw_cp.wait()
    wide[...] = raw[...].astype(F32)
    for kind in (1, 0, 2):
        for hh in range(4):
            qkvt[kind, hh] = wide[pl.ds(kind * 4 + hh, HD, stride=12), :].astype(BF16)
    for kind in range(2):
        kvb[kind, h, k] = qkvt[1 + kind, h]
    qb[h] = qkvt[0, h]
    pl.semaphore_wait(barrier, len(everyone))

    def send(src, dst, rsem, dev):
        cp = pltpu.make_async_remote_copy(
            src_ref=src, dst_ref=dst, send_sem=ssem.at[0], recv_sem=rsem, device_id=dev, device_id_type=MESH
        )
        cp.start()
        return cp

    def received(ref, rsem):
        pltpu.make_async_remote_copy(
            src_ref=ref, dst_ref=ref, send_sem=ssem.at[0], recv_sem=rsem, device_id=core_dev, device_id_type=MESH
        ).wait_recv()

    def p1_send(kind, dst, o, sem):
        return send(qkvt.at[kind, (h + o) % 4], dst, p1r.at[sem], heads_dev[o])

    p2 = {}

    def p2_send(kv, role, o, member, dev):
        part = kvb.at[kv, (h + 4 - o) % 4, member]
        if dev is core_dev:
            send(part, part, p2c.at[kv], dev)
        else:
            p2[kv, role, o] = send(part, part, p2r.at[kv, role, o], dev)

    def p2_own(kv, o):
        p2_send(kv, 0, o, k, group[0])
        p2_send(kv, 1, o, k, group[1])
        p2_send(kv, 2, o, k, core_dev)

    def p2_forward(kv, o):
        first = 1 if kv == 0 and o < 2 else 0
        for side in (first, 1 - first):
            p2[kv, side, o].wait_recv()
            member = group_chip[side] * 2 + c
            if side == first:
                p2_send(kv, 2, o, member, group[1 - first])
            p2_send(kv, 3, o, member, core_dev)

    def p2_last(kv, o):
        p2[kv, 2, o].wait_recv()
        p2_send(kv, 3, o, group_chip[2] * 2 + c, core_dev)

    def p2_wait(kv):
        received(kvb.at[kv, :, pl.ds(0, 4)], p2c.at[kv])

    lo = pl.ds(0, HALF)
    hi = pl.ds(HALF, HALF)
    ty = x * 2 + 1 - yl

    def a1_send(src, t, half, sem, dev):
        return send(src.at[:, half], g.at[t, :, half], a1r.at[sem], dev)

    def a1_forward(i, other):
        received(g.at[0, :, lo], a1r.at[i])
        t = ((x + 3) % 4) * 2 + other
        a1_send(g.at[t], t, lo, 6, x_dev[1])
        received(g.at[0, :, hi], a1r.at[i + 1])
        t = ((x + 1) % 4) * 2 + other
        a1_send(g.at[t], t, hi, 6, x_dev[3])

    p1k = {}
    for o in (1, 3, 2):
        p1k[o] = p1_send(1, kvb.at[0, h, k], o, o - 1)
    a1_send(go, tp, lo, 2, x_dev[1])
    a1_send(go, tp, hi, 3, x_dev[3])
    a1_send(go, tp, lo, 0, y_dev)
    a1_send(go, tp, hi, 1, y_dev)
    a1_send(go, tp, hi, 6, x_dev[1])
    a1_send(go, tp, lo, 6, x_dev[3])
    p2_own(0, 0)
    for o in (1, 3):
        p1k[o].wait_recv()
        p2_own(0, o)
    p1v = {}
    for o in (1, 3, 2):
        p1v[o] = p1_send(2, kvb.at[1, h, k], o, 2 + o)
    a1_forward(2, yl)
    received(g.at[0, :, lo], a1r.at[0])
    a1_send(g.at[ty], ty, lo, 4, x_dev[1])
    p1k[2].wait_recv()
    p2_own(0, 2)
    for o in (1, 3, 2):
        p1_send(0, qb.at[h], o, 6)
    received(g.at[0, :, hi], a1r.at[1])
    a1_send(g.at[ty], ty, hi, 5, x_dev[3])
    a1_send(g.at[ty], ty, hi, 6, x_dev[1])
    a1_send(g.at[ty], ty, lo, 6, x_dev[3])
    for o in (0, 1, 3, 2):
        p2_forward(0, o)
    p2_own(1, 0)
    for o in (1, 3, 2):
        p1v[o].wait_recv()
        p2_own(1, o)
    a1_forward(4, 1 - yl)
    p2_forward(1, 0)
    for o in (0, 1, 3, 2):
        p2_last(0, o)
    for o in (1, 3, 2):
        p2_forward(1, o)
    received(qb.at[pl.ds(0, 3)], p1r.at[6])
    p2_wait(0)

    col_max = [None] * 4
    key_pos = lax.broadcasted_iota(jnp.int32, (1024, HD), 0)
    row_pos = k * HD + lax.broadcasted_iota(jnp.int32, (1024, HD), 1)
    for j in range(4):
        rows = 512 - HD * j
        s = dot(kvb[0, j].reshape(1024, HD), qb[pl.ds(j, 4 - j)].reshape(rows, HD), NT) * factor
        first = jnp.where(key_pos <= row_pos, s[:, :HD], -jnp.inf)
        s = first if rows == HD else jnp.concatenate([first, s[:, HD:]], axis=1)
        st[j, :, HD * j :] = s
        m = jnp.max(s, axis=0, keepdims=True)
        for i in range(j, 4):
            part = m[:, (i - j) * HD : (i - j + 1) * HD]
            col_max[i] = part if col_max[i] is None else jnp.maximum(col_max[i], part)
    m_all = jnp.concatenate(col_max, axis=1)
    total = [None] * 4
    for j in range(4):
        p = jnp.exp(st[j, :, HD * j :] - m_all[:, HD * j :])
        st[j, :, HD * j :] = p
        m = jnp.sum(p, axis=0, keepdims=True)
        for i in range(j, 4):
            part = m[:, (i - j) * HD : (i - j + 1) * HD]
            total[i] = part if total[i] is None else total[i] + part
    inv = 1.0 / jnp.concatenate(total, axis=1)
    for o in (0, 1, 3, 2):
        p2_last(1, o)
    p2_wait(1)
    for j in range(4):
        p = st[j, :, HD * j :] * inv[:, HD * j :]
        st[j, :, HD * j :] = p
        p_low = p.astype(BF16)
        wl[j, :, HD * j :] = p_low
        o_t = dot(kvb[1, j].reshape(1024, HD), p_low, TN)
        if j == 0:
            ot[...] = o_t
        else:
            ot[:, HD * j :] += o_t
    o_low = ot[...].astype(BF16).astype(F32)
    asend[...] = o_low.T.astype(BF16).reshape(4, HD, HD)
    for o in (1, 3, 2):
        send(asend.at[(h + o) % 4], ah.at[h], atr.at[0], heads_dev[o])
    ah[h] = asend[h]

    g_cp.wait()
    w_cp.wait()
    received(g.at[pl.ds(0, 4)], a1r.at[6])
    gatt = dot(g[...].reshape(HD, D), w[...], NT).astype(BF16)
    for hh in range(4):
        gs[hh] = gatt[:, hh * HD : (hh + 1) * HD]
    for o in (1, 3, 2):
        send(gs.at[(h + o) % 4], gb.at[h], gtr.at[0], heads_dev[o])
    gb[h] = gs[h]

    c1 = {}

    def home_send(src, local, rsem, j):
        @pl.when(h != j)
        def _():
            send(src, local, rsem, (8 * j + k, tp))

        @pl.when(h == j)
        def _():
            local[...] = src[...]

    def backward(j):
        rows = 512 - HD * j
        q = qb[pl.ds(j, 4 - j)].reshape(rows, HD)
        ga = gb[pl.ds(j, 4 - j)].reshape(rows, HD)
        delta_j = delta[:, HD * j :]

        dp = dot(kvb[1, j].reshape(1024, HD), ga, NT)
        ds = (st[j, :, HD * j :] * (dp - delta_j) * factor).astype(BF16)
        dsb[:, HD * j :] = ds
        dkv[j, 0] = dot(ds, q, NN).reshape(8, HD, HD)
        dkv[j, 1] = dot(wl[j, :, HD * j :], ga, NN).reshape(8, HD, HD)
        keys = kvb[0, j].reshape(1024, HD)
        dq_t = dot(keys, dsb[:, HD * j :], TN)
        if j == 0:
            dqt[...] = dq_t
        else:
            dqt[:, HD * j :] += dq_t
        for mm in range(4):
            for kv in range(2):
                sb1[j, mm, kv] = dkv[j, kv, mm * 2 + 1 - c].astype(BF16)
        c1[j] = send(sb1.at[j], rb1.at[j], c1r.at[j], core_dev)
        sbq[j] = dqt[:, HD * j : HD * (j + 1)].T.astype(BF16)
        home_send(sbq.at[j], hq.at[h], dqr.at[0], j)

    def of_chip(j, kv, mp):
        return dkv[j, kv, mp * 2 + c] + rb1[j, mp, kv].astype(F32)

    def chip_sum(j):
        c1[j].wait_recv()
        for kv in range(2):
            s2a[j, kv, 0] = of_chip(j, kv, group_chip[kv]).astype(BF16)
            s2a[j, kv, 1] = of_chip(j, kv, group_chip[2]).astype(BF16)
            send(s2a.at[j, kv], r2a.at[j, kv], c2r.at[0, j], group[kv])

    def relay(j):
        received(r2a.at[j], c2r.at[0, j])
        for kv in range(2):
            s2b[j, kv] = (of_chip(j, kv, group_chip[1 - kv]) + r2a[j, kv, 1].astype(F32)).astype(BF16)
            send(s2b.at[j, kv], r2b.at[j, kv], c2r.at[1, j], group[1 - kv])

    def finish(j):
        received(r2b.at[j], c2r.at[1, j])
        for kv in range(2):
            v = of_chip(j, kv, chip) + r2a[j, kv, 0].astype(F32) + r2b[j, kv].astype(F32)
            sb3[j, kv] = v.astype(BF16)
        home_send(sb3.at[j], hb.at[h], c3r.at[0], j)

    m_cp = {}
    xr, xo, xl = (x + 1) % 4, (x + 2) % 4, (x + 3) % 4

    def m_send(n, i, src, dst, dev):
        m_cp[n, i] = send(src, dst, mr.at[n, i], dev)

    def project(n):
        for half in range(2):
            cols = pl.ds(n * PC + half * PH, PH)
            r = dot(att, w[:, cols], NN).reshape(4, 2, 16, PH)
            mf[:, :, :, cols] = r
            mb[:, :, :, cols] = r.astype(BF16)

    def first_hop(n):
        left = pl.ds(n * PC, PH)
        right = pl.ds(n * PC + PH, PH)
        m_send(n, 0, mb.at[xo, :, :, left], r1l.at[n], x_dev[1])
        m_send(n, 1, mb.at[xo, :, :, right], r1h.at[n], x_dev[3])

    def direct(n):
        left = pl.ds(n * PC, PH)
        right = pl.ds(n * PC + PH, PH)
        m_send(n, 2, mb.at[xr, :, :, right], rx.at[n, 0, :, :, pl.ds(PH, PH)], x_dev[1])
        m_send(n, 2, mb.at[xl, :, :, left], rx.at[n, 1, :, :, pl.ds(0, PH)], x_dev[3])

    def pass_on(n):
        m_cp[n, 0].wait_recv()
        accl[n] = (mf[xr, :, :, pl.ds(n * PC, PH)] + r1l[n].astype(F32)).astype(BF16)
        m_send(n, 2, accl.at[n], rx.at[n, 0, :, :, pl.ds(0, PH)], x_dev[1])
        m_cp[n, 1].wait_recv()
        acch[n] = (mf[xl, :, :, pl.ds(n * PC + PH, PH)] + r1h[n].astype(F32)).astype(BF16)
        m_send(n, 2, acch.at[n], rx.at[n, 1, :, :, pl.ds(PH, PH)], x_dev[3])

    last = PIECES - 1
    cols_a = pl.ds(last * PC, PC)

    def a_over_y():
        m_send(last, 3, mb.at[:, 1 - yl, :, cols_a], ra, y_dev)

    def a_first_hop():
        m_cp[last, 3].wait_recv()
        for i in range(4):
            v = mf[i, yl, :, cols_a] + ra[i].astype(F32)
            mf[i, yl, :, cols_a] = v
            sa[i] = v.astype(BF16)
        m_send(last, 0, sa.at[xo, :, pl.ds(0, PH)], r1a.at[0], x_dev[1])
        m_send(last, 1, sa.at[xo, :, pl.ds(PH, PH)], r1a.at[1], x_dev[3])
        m_send(last, 2, sa.at[xr, :, pl.ds(PH, PH)], rxa.at[0, :, pl.ds(PH, PH)], x_dev[1])
        m_send(last, 2, sa.at[xl, :, pl.ds(0, PH)], rxa.at[1, :, pl.ds(0, PH)], x_dev[3])

    def a_pass_on():
        m_cp[last, 0].wait_recv()
        acca[0] = (mf[xr, yl, :, pl.ds(last * PC, PH)] + r1a[0].astype(F32)).astype(BF16)
        m_send(last, 2, acca.at[0], rxa.at[0, :, pl.ds(0, PH)], x_dev[1])
        m_cp[last, 1].wait_recv()
        acca[1] = (mf[xl, yl, :, pl.ds(last * PC + PH, PH)] + r1a[1].astype(F32)).astype(BF16)
        m_send(last, 2, acca.at[1], rxa.at[1, :, pl.ds(PH, PH)], x_dev[3])

    def a_last_sum():
        received(rxa, mr.at[last, 2])
        mo[:, cols_a] = mf[x, yl, :, cols_a] + rxa[0].astype(F32) + rxa[1].astype(F32)
        out(mo.at[:, cols_a], mixed.at[:, cols_a], 0)

    def x_total(n, y):
        return mf[x, y, :, pl.ds(n * PC, PC)] + rx[n, 0, y].astype(F32) + rx[n, 1, y].astype(F32)

    def over_y(n):
        received(rx.at[n], mr.at[n, 2])
        sy[n] = x_total(n, 1 - yl).astype(BF16)
        m_send(n, 3, sy.at[n], ry.at[n], y_dev)

    def out(src, dst, i):
        pltpu.make_async_copy(src, dst, osem.at[i]).start()

    def last_sum(n):
        v = x_total(n, yl)
        m_cp[n, 3].wait_recv()
        cols = pl.ds(n * PC, PC)
        mo[:, cols] = v + ry[n].astype(F32)
        out(mo.at[:, cols], mixed.at[:, cols], 0)

    received(asend.at[pl.ds(0, 3)], atr.at[0])
    att = jnp.concatenate([ah[i] for i in range(4)], axis=1)
    project(last)
    a_over_y()
    for n in range(last):
        project(n)
        first_hop(n)
    direct(0)
    direct(1)
    received(gs.at[pl.ds(0, 3)], gtr.at[0])
    g_t = gb[...].reshape(512, HD).astype(F32).T
    delta = jnp.sum(g_t * o_low, axis=0, keepdims=True)
    backward(0)
    backward(1)
    chip_sum(0)
    backward(2)
    chip_sum(1)
    backward(3)
    pass_on(0)
    direct(2)
    chip_sum(2)
    pass_on(1)
    chip_sum(3)
    pass_on(2)
    relay(0)
    a_first_hop()
    relay(1)
    over_y(0)
    relay(2)
    relay(3)
    finish(0)
    a_pass_on()
    finish(1)
    over_y(1)
    finish(2)
    over_y(2)
    finish(3)
    for n in range(last):
        last_sum(n)
    a_last_sum()
    received(sbq.at[pl.ds(0, 3)], dqr.at[0])
    out(hq, dq_out, 1)
    received(sb3.at[pl.ds(0, 3)], c3r.at[0])
    out(hb, dkv_out, 2)

    everything = w.at[pl.ds(0, 496)]
    pltpu.make_async_remote_copy(
        src_ref=everything, dst_ref=everything, send_sem=ssem.at[0], recv_sem=p1r.at[0],
        device_id=core_dev, device_id_type=MESH,
    ).wait_send()
    pltpu.make_async_copy(mo, mixed, osem.at[0]).wait()
    pltpu.make_async_copy(hq, dq_out, osem.at[1]).wait()
    pltpu.make_async_copy(hb, dkv_out, osem.at[2]).wait()


def finish_kernel(mixed_in, dq, dkv, mixed, rows_out, rows, sem):
    copies = [pltpu.make_async_copy(mixed_in, mixed, sem.at[0])]
    copies[0].start()
    n = 32
    for part in range(HD // n):
        pos = pl.ds(part * n, n)
        for i in range(4):
            for kind in range(3):
                v = dq[i, pos] if kind == 0 else dkv[i, kind - 1, pos]
                rows[pl.ds(part * n * 12 + kind * 4 + i, n, stride=12), :] = v.astype(F32)
        span = pl.ds(part * n * 12, n * 12)
        copies.append(pltpu.make_async_copy(rows.at[span], rows_out.at[span], sem.at[1 + part]))
        copies[-1].start()
    for cp in copies:
        cp.wait()


def per_device(qkv, grad_out, attn_out):
    dma = pltpu.SemaphoreType.DMA
    vm = pltpu.VMEM
    scratch = [
        vm((1536, HD), BF16),
        vm((1536, HD), F32),
        vm((3, 4, HD, HD), BF16),
        vm((512, D), BF16),
        vm((8, 16, D), BF16),
        vm((2, 4, 8, HD, HD), BF16),
        vm((4, HD, HD), BF16),
        vm((4, 1024, 512), F32),
        vm((4, 1024, 512), BF16),
        vm((1024, 512), BF16),
        vm((HD, 512), F32),
        vm((HD, 512), F32),
        vm((4, HD, HD), BF16),
        vm((4, HD, HD), BF16),
        vm((4, HD, HD), BF16),
        vm((4, HD, HD), BF16),
        vm((4, 2, 8, HD, HD), F32),
        vm((4, 4, 2, HD, HD), BF16),
        vm((4, 4, 2, HD, HD), BF16),
        vm((4, 2, 2, HD, HD), BF16),
        vm((4, 2, 2, HD, HD), BF16),
        vm((4, 2, HD, HD), BF16),
        vm((4, 2, HD, HD), BF16),
        vm((4, 2, HD, HD), BF16),
        vm((4, 2, HD, HD), BF16),
        vm((4, HD, HD), BF16),
        vm((4, HD, HD), BF16),
        vm((4, 2, 16, D), F32),
        vm((4, 2, 16, D), BF16),
        vm((PIECES - 1, 2, 16, PH), BF16),
        vm((PIECES - 1, 2, 16, PH), BF16),
        vm((PIECES - 1, 2, 16, PH), BF16),
        vm((PIECES - 1, 2, 16, PH), BF16),
        vm((PIECES - 1, 2, 2, 16, PC), BF16),
        vm((PIECES - 1, 16, PC), BF16),
        vm((PIECES - 1, 16, PC), BF16),
        vm((4, 16, PC), BF16),
        vm((4, 16, PC), BF16),
        vm((2, 16, PH), BF16),
        vm((2, 16, PH), BF16),
        vm((2, 16, PC), BF16),
        vm((16, D), F32),
        dma((3,)),
        dma((1,)),
        dma((7,)),
        dma((2, 3, 4)), dma((2,)),
        dma((7,)),
        dma((1,)), dma((1,)),
        dma((4,)), dma((2, 4)),
        dma((1,)), dma((1,)),
        dma((PIECES, 4)),
        dma((3,)),
    ]
    rows = qkv.transpose(0, 2, 1, 3).reshape(1536, HD)
    mixed, dq, dkv = pl.pallas_call(
        kernel,
        out_shape=(
            jax.ShapeDtypeStruct((16, D), F32),
            jax.ShapeDtypeStruct((4, HD, HD), BF16),
            jax.ShapeDtypeStruct((4, 2, HD, HD), BF16),
        ),
        in_specs=[pl.BlockSpec(memory_space=pl.ANY)] * 3,
        out_specs=[pl.BlockSpec(memory_space=pl.ANY)] * 3,
        scratch_shapes=scratch,
        compiler_params=pltpu.CompilerParams(
            collective_id=0, has_side_effects=True, vmem_limit_bytes=60 * 1024 * 1024
        ),
    )(rows, grad_out, attn_out)
    mixed, grads = pl.pallas_call(
        finish_kernel,
        out_shape=(
            jax.ShapeDtypeStruct((16, D), F32),
            jax.ShapeDtypeStruct((1536, HD), F32),
        ),
        in_specs=[pl.BlockSpec(memory_space=pltpu.VMEM)] * 3,
        out_specs=[pl.BlockSpec(memory_space=pl.ANY)] * 2,
        scratch_shapes=[pltpu.VMEM((1536, HD), F32), pltpu.SemaphoreType.DMA((5,))],
    )(mixed, dq, dkv)
    return mixed, grads.reshape(HD, 3, 4, HD).transpose(0, 2, 1, 3)


def solution(mesh):
    in_specs = (P("ctx", "tp", None, None), P(("ctx", "tp"), None), P("tp", None))
    out_specs = (P(("ctx", "tp"), None), P("ctx", "tp", None, None))
    return jax.shard_map(
        per_device, mesh=mesh, in_specs=in_specs, out_specs=out_specs, check_vma=False
    )
```

```python
import functools
import math

import jax
import jax.numpy as jnp
from jax import lax
from jax.experimental import pallas as pl
from jax.experimental.pallas import tpu as pltpu
from jax.sharding import PartitionSpec as P

HD = 128
MESH = pl.DeviceIdType.MESH
F32 = jnp.float32
BF16 = jnp.bfloat16
D = 8192
HALF = D // 2
PIECES = 4
PC = D // PIECES
PH = PC // 2
NT = (((1,), (1,)), ((), ()))
TN = (((0,), (0,)), ((), ()))
NN = (((1,), (0,)), ((), ()))


def dot(a, b, dims):
    return lax.dot_general(a, b, dims, preferred_element_type=F32)


def kernel(
    qkv, go, wo,
    mixed, dq_out, dkv_out,
    raw, wide, qkvt, w, g, kvb, qb, st, wl, dsb, ot, dqt, gs, gb, asend, ah,
    dkv, sb1, rb1, s2a, r2a, s2b, r2b, sb3, hb, sbq, hq,
    mf, mb, r1l, r1h, accl, acch, rx, sy, ry, ra, sa, r1a, acca, rxa, mo, gacc,
    lsem, ssem, p1r, p2r, p2c, a1r, gtr, atr, c1r, c2r, c3r, dqr, mr, osem,
):
    ctx = lax.axis_index("ctx")
    tp = lax.axis_index("tp")
    h = ctx // 8
    k = ctx % 8
    zb = k // 4
    yh = (k // 2) % 2
    c = k % 2
    x = tp // 2
    yl = tp % 2
    chip = k // 2
    factor = 1.0 / math.sqrt(HD)

    heads_dev = {o: (((h + o) % 4) * 8 + k, tp) for o in (1, 2, 3)}
    core_dev = (ctx + 1 - 2 * c, tp)
    group = [
        (ctx + 4 - 8 * zb, tp),
        (ctx + 2 - 4 * yh, tp),
        (ctx + 6 - 8 * zb - 4 * yh, tp),
    ]
    group_chip = [chip + 2 - 4 * zb, chip + 1 - 2 * yh, 3 - chip]
    x_dev = {d: (ctx, ((x + d) % 4) * 2 + yl) for d in (1, 2, 3)}
    y_dev = (ctx, x * 2 + 1 - yl)

    raw_cp = pltpu.make_async_copy(qkv, raw, lsem.at[1])
    raw_cp.start()
    g_cp = pltpu.make_async_copy(go, g.at[tp], lsem.at[2])
    g_cp.start()
    w_cp = pltpu.make_async_copy(wo, w, lsem.at[0])
    w_cp.start()

    everyone = list(heads_dev.values()) + [core_dev] + group + list(x_dev.values()) + [y_dev]
    barrier = pltpu.get_barrier_semaphore()
    for dev in everyone:
        pl.semaphore_signal(barrier, inc=1, device_id=dev, device_id_type=MESH)
    raw_cp.wait()
    wide[...] = raw[...].astype(F32)
    for kind in (1, 0, 2):
        for hh in range(4):
            qkvt[kind, hh] = wide[pl.ds(kind * 4 + hh, HD, stride=12), :].astype(BF16)
    for kind in range(2):
        kvb[kind, h, k] = qkvt[1 + kind, h]
    qb[h] = qkvt[0, h]
    pl.semaphore_wait(barrier, len(everyone))

    def send(src, dst, rsem, dev):
        cp = pltpu.make_async_remote_copy(
            src_ref=src, dst_ref=dst, send_sem=ssem.at[0], recv_sem=rsem, device_id=dev, device_id_type=MESH
        )
        cp.start()
        return cp

    def received(ref, rsem):
        pltpu.make_async_remote_copy(
            src_ref=ref, dst_ref=ref, send_sem=ssem.at[0], recv_sem=rsem, device_id=core_dev, device_id_type=MESH
        ).wait_recv()

    def p1_send(kind, dst, o, sem):
        return send(qkvt.at[kind, (h + o) % 4], dst, p1r.at[sem], heads_dev[o])

    p2 = {}

    def p2_send(kv, role, o, member, dev):
        part = kvb.at[kv, (h + 4 - o) % 4, member]
        if dev is core_dev:
            send(part, part, p2c.at[kv], dev)
        else:
            p2[kv, role, o] = send(part, part, p2r.at[kv, role, o], dev)

    def p2_own(kv, o):
        p2_send(kv, 0, o, k, group[0])
        p2_send(kv, 1, o, k, group[1])
        p2_send(kv, 2, o, k, core_dev)

    def p2_forward(kv, o):
        first = 1 if kv == 0 and o < 2 else 0
        for side in (first, 1 - first):
            p2[kv, side, o].wait_recv()
            member = group_chip[side] * 2 + c
            if side == first:
                p2_send(kv, 2, o, member, group[1 - first])
            p2_send(kv, 3, o, member, core_dev)

    def p2_last(kv, o):
        p2[kv, 2, o].wait_recv()
        p2_send(kv, 3, o, group_chip[2] * 2 + c, core_dev)

    def p2_wait(kv):
        received(kvb.at[kv, :, pl.ds(0, 4)], p2c.at[kv])

    lo = pl.ds(0, HALF)
    hi = pl.ds(HALF, HALF)
    ty = x * 2 + 1 - yl

    def a1_send(src, t, half, sem, dev):
        return send(src.at[:, half], g.at[t, :, half], a1r.at[sem], dev)

    def a1_forward(i, other):
        received(g.at[0, :, lo], a1r.at[i])
        t = ((x + 3) % 4) * 2 + other
        a1_send(g.at[t], t, lo, 6, x_dev[1])
        received(g.at[0, :, hi], a1r.at[i + 1])
        t = ((x + 1) % 4) * 2 + other
        a1_send(g.at[t], t, hi, 6, x_dev[3])

    p1k = {}
    for o in (1, 3, 2):
        p1k[o] = p1_send(1, kvb.at[0, h, k], o, o - 1)
    a1_send(go, tp, lo, 2, x_dev[1])
    a1_send(go, tp, hi, 3, x_dev[3])
    a1_send(go, tp, lo, 0, y_dev)
    a1_send(go, tp, hi, 1, y_dev)
    a1_send(go, tp, hi, 6, x_dev[1])
    a1_send(go, tp, lo, 6, x_dev[3])
    p2_own(0, 0)
    for o in (1, 3):
        p1k[o].wait_recv()
        p2_own(0, o)
    p1v = {}
    for o in (1, 3, 2):
        p1v[o] = p1_send(2, kvb.at[1, h, k], o, 2 + o)
    a1_forward(2, yl)
    received(g.at[0, :, lo], a1r.at[0])
    a1_send(g.at[ty], ty, lo, 4, x_dev[1])
    p1k[2].wait_recv()
    p2_own(0, 2)
    for o in (1, 3, 2):
        p1_send(0, qb.at[h], o, 6)
    received(g.at[0, :, hi], a1r.at[1])
    a1_send(g.at[ty], ty, hi, 5, x_dev[3])
    a1_send(g.at[ty], ty, hi, 6, x_dev[1])
    a1_send(g.at[ty], ty, lo, 6, x_dev[3])
    for o in (0, 1, 3, 2):
        p2_forward(0, o)
    p2_own(1, 0)
    for o in (1, 3, 2):
        p1v[o].wait_recv()
        p2_own(1, o)
    a1_forward(4, 1 - yl)
    p2_forward(1, 0)
    for o in (0, 1, 3, 2):
        p2_last(0, o)
    for o in (1, 3, 2):
        p2_forward(1, o)
    received(qb.at[pl.ds(0, 3)], p1r.at[6])
    p2_wait(0)

    col_max = [None] * 4
    key_pos = lax.broadcasted_iota(jnp.int32, (1024, HD), 0)
    row_pos = k * HD + lax.broadcasted_iota(jnp.int32, (1024, HD), 1)
    for j in range(4):
        rows = 512 - HD * j
        s = dot(kvb[0, j].reshape(1024, HD), qb[pl.ds(j, 4 - j)].reshape(rows, HD), NT) * factor
        first = jnp.where(key_pos <= row_pos, s[:, :HD], -jnp.inf)
        s = first if rows == HD else jnp.concatenate([first, s[:, HD:]], axis=1)
        st[j, :, HD * j :] = s
        m = jnp.max(s, axis=0, keepdims=True)
        for i in range(j, 4):
            part = m[:, (i - j) * HD : (i - j + 1) * HD]
            col_max[i] = part if col_max[i] is None else jnp.maximum(col_max[i], part)
    m_all = jnp.concatenate(col_max, axis=1)
    total = [None] * 4
    for j in range(4):
        p = jnp.exp(st[j, :, HD * j :] - m_all[:, HD * j :])
        st[j, :, HD * j :] = p
        m = jnp.sum(p, axis=0, keepdims=True)
        for i in range(j, 4):
            part = m[:, (i - j) * HD : (i - j + 1) * HD]
            total[i] = part if total[i] is None else total[i] + part
    inv = 1.0 / jnp.concatenate(total, axis=1)
    for o in (0, 1, 3, 2):
        p2_last(1, o)
    g_cp.wait()
    w_cp.wait()
    received(g.at[pl.ds(0, 4)], a1r.at[6])
    gacc[...] = dot(g[:, :, :HALF].reshape(HD, HALF), w[:, :HALF], NT)
    p2_wait(1)
    for j in range(4):
        p = st[j, :, HD * j :] * inv[:, HD * j :]
        st[j, :, HD * j :] = p
        p_low = p.astype(BF16)
        wl[j, :, HD * j :] = p_low
        o_t = dot(kvb[1, j].reshape(1024, HD), p_low, TN)
        if j == 0:
            ot[...] = o_t
        else:
            ot[:, HD * j :] += o_t
    o_low = ot[...].astype(BF16).astype(F32)
    asend[...] = o_low.T.astype(BF16).reshape(4, HD, HD)
    for o in (1, 3, 2):
        send(asend.at[(h + o) % 4], ah.at[h], atr.at[0], heads_dev[o])
    ah[h] = asend[h]

    gatt = (gacc[...] + dot(g[:, :, HALF:].reshape(HD, HALF), w[:, HALF:], NT)).astype(BF16)
    for hh in range(4):
        gs[hh] = gatt[:, hh * HD : (hh + 1) * HD]
    for o in (1, 3, 2):
        send(gs.at[(h + o) % 4], gb.at[h], gtr.at[0], heads_dev[o])
    gb[h] = gs[h]

    c1 = {}

    def home_send(src, local, rsem, j):
        @pl.when(h != j)
        def _():
            send(src, local, rsem, (8 * j + k, tp))

        @pl.when(h == j)
        def _():
            local[...] = src[...]

    def backward(j):
        rows = 512 - HD * j
        q = qb[pl.ds(j, 4 - j)].reshape(rows, HD)
        ga = gb[pl.ds(j, 4 - j)].reshape(rows, HD)
        delta_j = delta[:, HD * j :]

        dp = dot(kvb[1, j].reshape(1024, HD), ga, NT)
        ds = (st[j, :, HD * j :] * (dp - delta_j) * factor).astype(BF16)
        dsb[:, HD * j :] = ds
        dkv[j, 0] = dot(ds, q, NN).reshape(8, HD, HD)
        dkv[j, 1] = dot(wl[j, :, HD * j :], ga, NN).reshape(8, HD, HD)
        keys = kvb[0, j].reshape(1024, HD)
        dq_t = dot(keys, dsb[:, HD * j :], TN)
        if j == 0:
            dqt[...] = dq_t
        else:
            dqt[:, HD * j :] += dq_t
        for mm in range(4):
            for kv in range(2):
                sb1[j, mm, kv] = dkv[j, kv, mm * 2 + 1 - c].astype(BF16)
        c1[j] = send(sb1.at[j], rb1.at[j], c1r.at[j], core_dev)
        sbq[j] = dqt[:, HD * j : HD * (j + 1)].T.astype(BF16)
        home_send(sbq.at[j], hq.at[h], dqr.at[0], j)

    def of_chip(j, kv, mp):
        return dkv[j, kv, mp * 2 + c] + rb1[j, mp, kv].astype(F32)

    def chip_sum(j):
        c1[j].wait_recv()
        for kv in range(2):
            s2a[j, kv, 0] = of_chip(j, kv, group_chip[kv]).astype(BF16)
            s2a[j, kv, 1] = of_chip(j, kv, group_chip[2]).astype(BF16)
            send(s2a.at[j, kv], r2a.at[j, kv], c2r.at[0, j], group[kv])

    def relay(j):
        received(r2a.at[j], c2r.at[0, j])
        for kv in range(2):
            s2b[j, kv] = (of_chip(j, kv, group_chip[1 - kv]) + r2a[j, kv, 1].astype(F32)).astype(BF16)
            send(s2b.at[j, kv], r2b.at[j, kv], c2r.at[1, j], group[1 - kv])

    def finish(j):
        received(r2b.at[j], c2r.at[1, j])
        for kv in range(2):
            v = of_chip(j, kv, chip) + r2a[j, kv, 0].astype(F32) + r2b[j, kv].astype(F32)
            sb3[j, kv] = v.astype(BF16)
        home_send(sb3.at[j], hb.at[h], c3r.at[0], j)

    m_cp = {}
    xr, xo, xl = (x + 1) % 4, (x + 2) % 4, (x + 3) % 4

    def m_send(n, i, src, dst, dev):
        m_cp[n, i] = send(src, dst, mr.at[n, i], dev)

    def project(n):
        for half in range(2):
            cols = pl.ds(n * PC + half * PH, PH)
            r = dot(att, w[:, cols], NN).reshape(4, 2, 16, PH)
            mf[:, :, :, cols] = r
            mb[:, :, :, cols] = r.astype(BF16)

    def first_hop(n):
        left = pl.ds(n * PC, PH)
        right = pl.ds(n * PC + PH, PH)
        m_send(n, 0, mb.at[xo, :, :, left], r1l.at[n], x_dev[1])
        m_send(n, 1, mb.at[xo, :, :, right], r1h.at[n], x_dev[3])

    def direct(n):
        left = pl.ds(n * PC, PH)
        right = pl.ds(n * PC + PH, PH)
        m_send(n, 2, mb.at[xr, :, :, right], rx.at[n, 0, :, :, pl.ds(PH, PH)], x_dev[1])
        m_send(n, 2, mb.at[xl, :, :, left], rx.at[n, 1, :, :, pl.ds(0, PH)], x_dev[3])

    def pass_on(n):
        m_cp[n, 0].wait_recv()
        accl[n] = (mf[xr, :, :, pl.ds(n * PC, PH)] + r1l[n].astype(F32)).astype(BF16)
        m_send(n, 2, accl.at[n], rx.at[n, 0, :, :, pl.ds(0, PH)], x_dev[1])
        m_cp[n, 1].wait_recv()
        acch[n] = (mf[xl, :, :, pl.ds(n * PC + PH, PH)] + r1h[n].astype(F32)).astype(BF16)
        m_send(n, 2, acch.at[n], rx.at[n, 1, :, :, pl.ds(PH, PH)], x_dev[3])

    last = PIECES - 1
    cols_a = pl.ds(last * PC, PC)

    def a_over_y():
        m_send(last, 3, mb.at[:, 1 - yl, :, cols_a], ra, y_dev)

    def a_first_hop():
        m_cp[last, 3].wait_recv()
        for i in range(4):
            v = mf[i, yl, :, cols_a] + ra[i].astype(F32)
            mf[i, yl, :, cols_a] = v
            sa[i] = v.astype(BF16)
        m_send(last, 0, sa.at[xo, :, pl.ds(0, PH)], r1a.at[0], x_dev[1])
        m_send(last, 1, sa.at[xo, :, pl.ds(PH, PH)], r1a.at[1], x_dev[3])
        m_send(last, 2, sa.at[xr, :, pl.ds(PH, PH)], rxa.at[0, :, pl.ds(PH, PH)], x_dev[1])
        m_send(last, 2, sa.at[xl, :, pl.ds(0, PH)], rxa.at[1, :, pl.ds(0, PH)], x_dev[3])

    def a_pass_on():
        m_cp[last, 0].wait_recv()
        acca[0] = (mf[xr, yl, :, pl.ds(last * PC, PH)] + r1a[0].astype(F32)).astype(BF16)
        m_send(last, 2, acca.at[0], rxa.at[0, :, pl.ds(0, PH)], x_dev[1])
        m_cp[last, 1].wait_recv()
        acca[1] = (mf[xl, yl, :, pl.ds(last * PC + PH, PH)] + r1a[1].astype(F32)).astype(BF16)
        m_send(last, 2, acca.at[1], rxa.at[1, :, pl.ds(PH, PH)], x_dev[3])

    def a_last_sum():
        received(rxa, mr.at[last, 2])
        mo[:, cols_a] = mf[x, yl, :, cols_a] + rxa[0].astype(F32) + rxa[1].astype(F32)
        out(mo.at[:, cols_a], mixed.at[:, cols_a], 0)

    def x_total(n, y):
        return mf[x, y, :, pl.ds(n * PC, PC)] + rx[n, 0, y].astype(F32) + rx[n, 1, y].astype(F32)

    def over_y(n):
        received(rx.at[n], mr.at[n, 2])
        sy[n] = x_total(n, 1 - yl).astype(BF16)
        m_send(n, 3, sy.at[n], ry.at[n], y_dev)

    def out(src, dst, i):
        pltpu.make_async_copy(src, dst, osem.at[i]).start()

    def last_sum(n):
        v = x_total(n, yl)
        m_cp[n, 3].wait_recv()
        cols = pl.ds(n * PC, PC)
        mo[:, cols] = v + ry[n].astype(F32)
        out(mo.at[:, cols], mixed.at[:, cols], 0)

    received(asend.at[pl.ds(0, 3)], atr.at[0])
    att = jnp.concatenate([ah[i] for i in range(4)], axis=1)
    project(last)
    a_over_y()
    for n in range(last):
        project(n)
        first_hop(n)
    direct(0)
    direct(1)
    received(gs.at[pl.ds(0, 3)], gtr.at[0])
    g_t = gb[...].reshape(512, HD).astype(F32).T
    delta = jnp.sum(g_t * o_low, axis=0, keepdims=True)
    backward(0)
    backward(1)
    chip_sum(0)
    backward(2)
    chip_sum(1)
    backward(3)
    pass_on(0)
    direct(2)
    chip_sum(2)
    pass_on(1)
    chip_sum(3)
    pass_on(2)
    a_first_hop()
    relay(0)
    relay(1)
    over_y(0)
    relay(2)
    relay(3)
    finish(0)
    a_pass_on()
    finish(1)
    over_y(1)
    finish(2)
    over_y(2)
    finish(3)
    for n in range(last):
        last_sum(n)
    a_last_sum()
    received(sbq.at[pl.ds(0, 3)], dqr.at[0])
    out(hq, dq_out, 1)
    received(sb3.at[pl.ds(0, 3)], c3r.at[0])
    out(hb, dkv_out, 2)

    everything = w.at[pl.ds(0, 496)]
    pltpu.make_async_remote_copy(
        src_ref=everything, dst_ref=everything, send_sem=ssem.at[0], recv_sem=p1r.at[0],
        device_id=core_dev, device_id_type=MESH,
    ).wait_send()
    pltpu.make_async_copy(mo, mixed, osem.at[0]).wait()
    pltpu.make_async_copy(hq, dq_out, osem.at[1]).wait()
    pltpu.make_async_copy(hb, dkv_out, osem.at[2]).wait()


def finish_kernel(mixed_in, dq, dkv, mixed, rows_out, rows, sem):
    copies = [pltpu.make_async_copy(mixed_in, mixed, sem.at[0])]
    copies[0].start()
    n = 32
    for part in range(HD // n):
        pos = pl.ds(part * n, n)
        for i in range(4):
            for kind in range(3):
                v = dq[i, pos] if kind == 0 else dkv[i, kind - 1, pos]
                rows[pl.ds(part * n * 12 + kind * 4 + i, n, stride=12), :] = v.astype(F32)
        span = pl.ds(part * n * 12, n * 12)
        copies.append(pltpu.make_async_copy(rows.at[span], rows_out.at[span], sem.at[1 + part]))
        copies[-1].start()
    for cp in copies:
        cp.wait()


def per_device(qkv, grad_out, attn_out):
    dma = pltpu.SemaphoreType.DMA
    vm = pltpu.VMEM
    scratch = [
        vm((1536, HD), BF16),
        vm((1536, HD), F32),
        vm((3, 4, HD, HD), BF16),
        vm((512, D), BF16),
        vm((8, 16, D), BF16),
        vm((2, 4, 8, HD, HD), BF16),
        vm((4, HD, HD), BF16),
        vm((4, 1024, 512), F32),
        vm((4, 1024, 512), BF16),
        vm((1024, 512), BF16),
        vm((HD, 512), F32),
        vm((HD, 512), F32),
        vm((4, HD, HD), BF16),
        vm((4, HD, HD), BF16),
        vm((4, HD, HD), BF16),
        vm((4, HD, HD), BF16),
        vm((4, 2, 8, HD, HD), F32),
        vm((4, 4, 2, HD, HD), BF16),
        vm((4, 4, 2, HD, HD), BF16),
        vm((4, 2, 2, HD, HD), BF16),
        vm((4, 2, 2, HD, HD), BF16),
        vm((4, 2, HD, HD), BF16),
        vm((4, 2, HD, HD), BF16),
        vm((4, 2, HD, HD), BF16),
        vm((4, 2, HD, HD), BF16),
        vm((4, HD, HD), BF16),
        vm((4, HD, HD), BF16),
        vm((4, 2, 16, D), F32),
        vm((4, 2, 16, D), BF16),
        vm((PIECES - 1, 2, 16, PH), BF16),
        vm((PIECES - 1, 2, 16, PH), BF16),
        vm((PIECES - 1, 2, 16, PH), BF16),
        vm((PIECES - 1, 2, 16, PH), BF16),
        vm((PIECES - 1, 2, 2, 16, PC), BF16),
        vm((PIECES - 1, 16, PC), BF16),
        vm((PIECES - 1, 16, PC), BF16),
        vm((4, 16, PC), BF16),
        vm((4, 16, PC), BF16),
        vm((2, 16, PH), BF16),
        vm((2, 16, PH), BF16),
        vm((2, 16, PC), BF16),
        vm((16, D), F32),
        vm((HD, 512), F32),
        dma((3,)),
        dma((1,)),
        dma((7,)),
        dma((2, 3, 4)), dma((2,)),
        dma((7,)),
        dma((1,)), dma((1,)),
        dma((4,)), dma((2, 4)),
        dma((1,)), dma((1,)),
        dma((PIECES, 4)),
        dma((3,)),
    ]
    rows = qkv.transpose(0, 2, 1, 3).reshape(1536, HD)
    mixed, dq, dkv = pl.pallas_call(
        kernel,
        out_shape=(
            jax.ShapeDtypeStruct((16, D), F32),
            jax.ShapeDtypeStruct((4, HD, HD), BF16),
            jax.ShapeDtypeStruct((4, 2, HD, HD), BF16),
        ),
        in_specs=[pl.BlockSpec(memory_space=pl.ANY)] * 3,
        out_specs=[pl.BlockSpec(memory_space=pl.ANY)] * 3,
        scratch_shapes=scratch,
        compiler_params=pltpu.CompilerParams(
            collective_id=0, has_side_effects=True, vmem_limit_bytes=60 * 1024 * 1024
        ),
    )(rows, grad_out, attn_out)
    mixed, grads = pl.pallas_call(
        finish_kernel,
        out_shape=(
            jax.ShapeDtypeStruct((16, D), F32),
            jax.ShapeDtypeStruct((1536, HD), F32),
        ),
        in_specs=[pl.BlockSpec(memory_space=pltpu.VMEM)] * 3,
        out_specs=[pl.BlockSpec(memory_space=pl.ANY)] * 2,
        scratch_shapes=[pltpu.VMEM((1536, HD), F32), pltpu.SemaphoreType.DMA((5,))],
    )(mixed, dq, dkv)
    return mixed, grads.reshape(HD, 3, 4, HD).transpose(0, 2, 1, 3)


def solution(mesh):
    in_specs = (P("ctx", "tp", None, None), P(("ctx", "tp"), None), P("tp", None))
    out_specs = (P(("ctx", "tp"), None), P("ctx", "tp", None, None))
    return jax.shard_map(
        per_device, mesh=mesh, in_specs=in_specs, out_specs=out_specs, check_vma=False
    )
```
